512 devices in a mesh: group: 16 (over x, y_hi, core), brick: 32 (over y_lo, z).
Axes of the slice: x: 4, y: 4 (y_hi: 2, y_lo: 2; y = y_hi * 2 + y_lo), z: 16, core: 2. Of those that a mesh axis runs over, the one named last changes fastest.
Arguments:
- field: float32 [32, 128, 16, 128], P('group', 'brick'), may hold values from -6 to 6
- cotangent: float32 [32, 128, 16, 128], P('group', 'brick'), may hold values from -6 to 6
- w_fine: bfloat16 [27, 128, 128], replicated, may hold values from -0.109375 to 0.109375
- w_coarse: bfloat16 [27, 128, 128], replicated, may hold values from -0.3125 to 0.3125
Outputs:
- output: float32 [32, 128, 16, 128], P('group', 'brick')
- grad_fine: float32 [27, 128, 128], P(None, 'brick')
- grad_coarse: float32 [27, 128, 128], P(None, 'brick')
The draws below stay inside these ranges and needn't reach their ends.
All inputs are finite; a program needn't handle non-finite values.
Results may differ from the reference program's by a relative error of at most 0.0053.
Values may be sent and summed in bfloat16 or wider, within the bound.
A program may use at most 64 MiB of HBM per device.

```python
import jax
import jax.numpy as jnp
from jax import lax

CH = 128
NZ = 16
NX = 32
NY = 128


def spiked(array, stream_key, source, target, parts, factor):
    owner, partner = [(jnp.arange(array.shape[position]) // (array.shape[position] // parts)).reshape([-1 if axis == position else 1 for axis in range(array.ndim)]) for position in (source, target)]
    chosen = jax.random.permutation(stream_key, parts)[partner]
    strong = (owner == chosen) | (owner == (partner + parts // 2) % parts)
    return jnp.where(strong, factor * array, array)


def shard_levels(rng, dims, split, low, high):
    factor_of = 1.0
    for dim, blocks in split:
        draws = jax.random.uniform(jax.random.fold_in(jax.random.fold_in(rng, 6), dim), (blocks,), jnp.float32, low / len(split), high / len(split))
        factor_of = factor_of * jnp.repeat(jnp.exp(draws), dims[dim] // blocks).reshape((-1,) + (1,) * (len(dims) - 1 - dim))
    return factor_of


def scatter_about(stream_key, dims, deviation, most, cuts=(), held_as=jnp.bfloat16):
    gain = shard_levels(stream_key, dims, cuts, -0.22, 0.18) if cuts else 1.0
    entries = jax.random.normal(stream_key, dims, jnp.float32) * deviation * gain
    return jnp.minimum(jnp.maximum(entries, -most), most).astype(held_as)


def bell_draw_with(stream_key, dims, scale, limit, cuts, heavy, held_as=jnp.bfloat16):
    entries = scale * jax.random.normal(stream_key, dims, jnp.float32)
    if cuts:
        entries = entries * shard_levels(stream_key, dims, cuts, -0.22, 0.18)
    return jnp.clip(spiked(entries, jax.random.fold_in(stream_key, 3), *heavy), -limit, limit).astype(held_as)


def setup_inputs(seed: int = 0) -> dict:
    splits = jax.random.split(jax.random.key(seed), 5)
    return {
        "field": bell_draw_with(splits[0], (NX, NY, NZ, CH), 1.0, 6.0, ((0, 16), (1, 32)), (1, 3, 32, 2.75), jnp.float32),
        "cotangent": scatter_about(splits[1], (NX, NY, NZ, CH), 1.0, 6.0, ((0, 16), (1, 32)), jnp.float32),
        "w_fine": scatter_about(splits[2], (27, CH, CH), (27 * CH) ** -0.5, 0.109375),
        "w_coarse": scatter_about(splits[3], (27, CH, CH), (27 * CH // 8) ** -0.5, 0.3125),
    }


def conv_padded(padded, weights):
    size_x = padded.shape[0] - 2
    size_y = padded.shape[1] - 2
    size_z = padded.shape[2] - 2
    channels = padded.shape[3]
    total = jnp.zeros((size_x * size_y * size_z, weights.shape[2]), jnp.float32)
    for offset in range(27):
        step_x, step_y, step_z = (offset // 9, offset // 3 % 3, offset % 3)
        window = padded[step_x:step_x + size_x, step_y:step_y + size_y, step_z:step_z + size_z].reshape(-1, channels)
        total = total + jnp.dot(window, weights[offset], preferred_element_type=jnp.float32)
    return total.reshape(size_x, size_y, size_z, -1)

def transposed(padded, weights):
    size_x = padded.shape[0] - 2
    size_y = padded.shape[1] - 2
    size_z = padded.shape[2] - 2
    channels = padded.shape[3]
    total = jnp.zeros((size_x * size_y * size_z, weights.shape[1]), jnp.float32)
    for offset in range(27):
        step_x, step_y, step_z = (2 - offset // 9, 2 - offset // 3 % 3, 2 - offset % 3)
        window = padded[step_x:step_x + size_x, step_y:step_y + size_y, step_z:step_z + size_z].reshape(-1, channels)
        total = total + lax.dot_general(window, weights[offset], (((1,), (1,)), ((), ())), preferred_element_type=jnp.float32)
    return total.reshape(size_x, size_y, size_z, -1)

def weight_grad(padded, grads):
    size_x, size_y, size_z, outputs = grads.shape
    channels = padded.shape[3]
    flat = grads.reshape(-1, outputs)
    pieces = []
    for offset in range(27):
        step_x, step_y, step_z = (offset // 9, offset // 3 % 3, offset % 3)
        window = padded[step_x:step_x + size_x, step_y:step_y + size_y, step_z:step_z + size_z].reshape(-1, channels)
        pieces.append(lax.dot_general(window, flat, (((0,), (0,)), ((), ())), preferred_element_type=jnp.float32))
    return jnp.stack(pieces)

def dsilu(values):
    sig = jax.nn.sigmoid(values)
    return sig * (1.0 + values * (1.0 - sig))

def pad_all(values):
    return jnp.pad(values, ((1, 1), (1, 1), (1, 1), (0, 0)))

def block_sum(values):
    size_x, size_y, size_z, channels = values.shape
    shaped = values.reshape(size_x // 2, 2, size_y // 2, 2, size_z // 2, 2, channels)
    return lax.optimization_barrier(jnp.sum(shaped, axis=(1, 3, 5)))

def expand(values):
    size_x, size_y, size_z, channels = values.shape
    wide = jnp.broadcast_to(values[:, None, :, None, :, None, :], (size_x, 2, size_y, 2, size_z, 2, channels))
    return wide.reshape(2 * size_x, 2 * size_y, 2 * size_z, channels)

def reference(field, cotangent, w_fine, w_coarse):
    fine_b = field.astype(jnp.bfloat16)
    fine_pad = pad_all(fine_b)
    z_fine = conv_padded(fine_pad, w_fine)
    act_fine = jax.nn.silu(z_fine)
    coarse = (block_sum(act_fine) * 0.125).astype(jnp.bfloat16)
    coarse_pad = pad_all(coarse)
    z_coarse = conv_padded(coarse_pad, w_coarse)
    act_coarse = jax.nn.silu(z_coarse)
    output = act_fine + expand(act_coarse)
    d_coarse = block_sum(cotangent)
    g_coarse = (d_coarse * dsilu(z_coarse)).astype(jnp.bfloat16)
    grad_coarse = weight_grad(coarse_pad, g_coarse)
    back_coarse = transposed(pad_all(g_coarse), w_coarse)
    g_fine = ((cotangent + expand(back_coarse) * 0.125) * dsilu(z_fine)).astype(jnp.bfloat16)
    grad_fine = weight_grad(fine_pad, g_fine)
    return (output, grad_fine, grad_coarse)
```

```python
import jax
import jax.numpy as jnp
from jax import lax
from jax.experimental import pallas as pl
from jax.experimental.pallas import tpu as pltpu
from jax.sharding import PartitionSpec as P

CH = 128
GROUPS = 16
BRICKS = 32
F32 = jnp.float32
BF16 = jnp.bfloat16
PART = 7


def wait_for(ref, sem):
    pltpu.make_async_copy(ref, ref, sem).wait()


def iota(shape, dim):
    return lax.broadcasted_iota(jnp.int32, shape, dim)


def neighbours_along_depth(rows, depth):
    count = rows.shape[0]
    place = iota(rows.shape, 0) & (depth - 1)
    before = jnp.where(place == 0, 0.0, pltpu.roll(rows, 1, 0))
    after = jnp.where(place == depth - 1, 0.0, pltpu.roll(rows, count - 1, 0))
    return before, after


def matmul_nt(a, b):
    return lax.dot_general(a, b, (((1,), (1,)), ((), ())), preferred_element_type=F32)


def pooled(values, pool):
    pool[...] = jnp.sum(values.reshape(2, 2, 2, 16, CH), axis=(0, 2)).reshape(32, CH)
    return pool[pl.ds(0, 16, stride=2), :] + pool[pl.ds(1, 16, stride=2), :]


def spread(values, pool):
    pool[pl.ds(0, 16, stride=2), :] = values
    pool[pl.ds(1, 16, stride=2), :] = values
    wide = jnp.broadcast_to(pool[...].reshape(1, 2, 1, 16, CH), (2, 2, 2, 16, CH))
    return wide.reshape(128, CH)


def selection(offset, rows, size_y, size_z):
    row = iota((rows, 128), 0)
    cell = iota((rows, 128), 1)
    step_x, step_y, step_z = offset // 9, (offset // 3) % 3, offset % 3
    plane = size_y * size_z
    z = cell % size_z + step_z - 1
    y = (cell // size_z) % size_y + step_y
    x = cell // plane + step_x
    source = (x * (size_y + 2) + y) * size_z + z
    inside = (z >= 0) & (z < size_z)
    if size_y == 2:
        inside = inside & (cell < plane)
    hit = inside & (row == source) & (offset < 27)
    return jnp.where(hit, 1.0, 0.0).astype(BF16)


def kernel(
    field, cot, w_fine, w_coarse, output, grad_fine, grad_coarse,
    field_v, cot_v, out_v, wf_v, wc_v, ext, ext3, pool, cext, gext,
    et_send, et_recv, ct_send, ct_recv, lf, lc, gf, gc, acc_f, acc_c,
    rows_f, rows_c, sum_f, sum_c, fin_f, fin_c,
    local_sem, send_sem, recv_sem,
):
    g = lax.axis_index("group")
    b = lax.axis_index("brick")
    g_up, g_down = (g + 1) % GROUPS, (g + GROUPS - 1) % GROUPS
    b_up, b_down = (b + 1) % BRICKS, (b + BRICKS - 1) % BRICKS
    share, quarter = g // 4, g % 4

    loads = [
        pltpu.make_async_copy(src, dst, local_sem.at[i])
        for i, (src, dst) in enumerate(((field, field_v), (cot, cot_v), (w_fine, wf_v), (w_coarse, wc_v)))
    ]
    for load in loads:
        load.start()

    barrier = pltpu.get_barrier_semaphore()

    def greet(group, brick):
        pl.semaphore_signal(barrier, inc=1, device_id=(group, brick), device_id_type=pl.DeviceIdType.MESH)

    for group in (g_up, g_down):
        for brick in (b_up, b_down):
            greet(group, brick)
    pl.loop(1, GROUPS)(lambda i: greet((g + i) % GROUPS, b))
    pl.loop(1, BRICKS)(lambda i: greet(g, (b + i) % BRICKS))

    def send(src, dst, phase, group, brick):
        pltpu.make_async_remote_copy(
            src_ref=src,
            dst_ref=dst,
            send_sem=send_sem.at[phase],
            recv_sem=recv_sem.at[phase],
            device_id=(group, brick),
            device_id_type=pl.DeviceIdType.MESH,
        ).start()

    loads[0].wait()
    ext[1:3, 1:5] = field_v[...].astype(BF16)
    pl.semaphore_wait(barrier, 4 + GROUPS - 1 + BRICKS - 1)

    send(ext.at[1, pl.ds(1, 4)], ext.at[3, pl.ds(1, 4)], 0, g_down, b)
    send(ext.at[2, pl.ds(1, 4)], ext.at[0, pl.ds(1, 4)], 0, g_up, b)
    send(ext.at[pl.ds(1, 2), 1], ext.at[pl.ds(1, 2), 5], 0, g, b_down)
    send(ext.at[pl.ds(1, 2), 4], ext.at[pl.ds(1, 2), 0], 0, g, b_up)
    send(ext.at[1, 1], ext.at[3, 5], 0, g_down, b_down)
    send(ext.at[1, 4], ext.at[3, 0], 0, g_down, b_up)
    send(ext.at[2, 1], ext.at[0, 5], 0, g_up, b_down)
    send(ext.at[2, 4], ext.at[0, 0], 0, g_up, b_up)

    loads[1].wait()
    cot_rows = cot_v[...].reshape(128, CH)
    d_coarse = pooled(cot_rows, pool)
    order = iota((CH, CH), 0)
    sort = jnp.where(iota((CH, CH), 1) == 4 * (order % 32) + order // 32, 1.0, 0.0).astype(BF16)

    wait_for(ext.at[pl.ds(0, 4), pl.ds(0, 4)], recv_sem.at[0])

    wait_for(ext.at[pl.ds(0, 4), pl.ds(0, 4)], send_sem.at[0])

    def clear(outside, part):
        @pl.when(outside)
        def _():
            ext[part] = jnp.zeros(ext.at[part].shape, BF16)

    clear(g == 0, slice(0, 1))
    clear(g == GROUPS - 1, slice(3, 4))
    clear(b == 0, (slice(0, 4), slice(0, 1)))
    clear(b == BRICKS - 1, (slice(0, 4), slice(5, 6)))

    cells = ext[...].reshape(384, CH)
    et_send[...] = matmul_nt(sort, cells).astype(BF16).reshape(4, 32, 384)
    et_recv[0] = et_send[share]

    @pl.loop(1, GROUPS)
    def _(i):
        to = (g + i) % GROUPS
        send(et_send.at[to // 4], et_recv.at[i], 1, to, b)

    before, after = neighbours_along_depth(cells.astype(F32), 16)
    ext3[:, :, :, 0:CH] = before.astype(BF16).reshape(4, 6, 16, CH)
    ext3[:, :, :, CH : 2 * CH] = ext[...]
    ext3[:, :, :, 2 * CH :] = after.astype(BF16).reshape(4, 6, 16, CH)

    loads[2].wait()
    z_fine = jnp.zeros((128, CH), F32)
    for step in range(9):
        step_x, step_y = step // 3, step % 3
        window = ext3[step_x : step_x + 2, step_y : step_y + 4].reshape(128, 3 * CH)
        z_fine = z_fine + jnp.dot(window, wf_v[step], preferred_element_type=F32)
    sig = jax.nn.sigmoid(z_fine)
    act_fine = z_fine * sig
    slope_fine = sig * (1.0 + z_fine * (1.0 - sig))
    coarse = (pooled(act_fine, pool) * 0.125).astype(BF16).astype(F32)

    def coarse_halo(buf, phase):
        send(buf.at[pl.ds(5, 2)], buf.at[pl.ds(9, 2)], phase, g_down, b)
        send(buf.at[pl.ds(5, 2)], buf.at[pl.ds(1, 2)], phase, g_up, b)
        send(buf.at[5], buf.at[7], phase, g, b_down)
        send(buf.at[6], buf.at[4], phase, g, b_up)
        send(buf.at[5], buf.at[11], phase, g_down, b_down)
        send(buf.at[6], buf.at[8], phase, g_down, b_up)
        send(buf.at[5], buf.at[3], phase, g_up, b_down)
        send(buf.at[6], buf.at[0], phase, g_up, b_up)

    def coarse_halo_wait(buf, phase):
        wait_for(buf.at[pl.ds(0, 10)], recv_sem.at[phase])
        wait_for(buf.at[pl.ds(0, 10)], send_sem.at[phase])

        def clear(outside, rows):
            @pl.when(outside)
            def _():
                for row in rows:
                    buf[row] = jnp.zeros((8, CH), F32)

        clear(g == 0, (0, 1, 2, 3))
        clear(g == GROUPS - 1, (8, 9, 10, 11))
        clear(b == 0, (0, 4, 8))
        clear(b == BRICKS - 1, (3, 7, 11))

    cext[5:7] = coarse.reshape(2, 8, CH)
    coarse_halo(cext, 2)
    coarse_halo_wait(cext, 2)

    ccells = cext[...].reshape(96, CH)
    before, after = neighbours_along_depth(ccells, 8)
    wide = jnp.concatenate([before, ccells, after], axis=1)
    loads[3].wait()
    z_coarse = jnp.zeros((16, CH), F32)
    for step in range(9):
        start = (step // 3) * 32 + (step % 3) * 8
        window = wide[start : start + 16].astype(BF16)
        z_coarse = z_coarse + jnp.dot(window, wc_v[step], preferred_element_type=F32)
    sig = jax.nn.sigmoid(z_coarse)
    act_coarse = z_coarse * sig
    g_coarse = d_coarse * (sig * (1.0 + z_coarse * (1.0 - sig)))
    g_coarse = g_coarse.astype(BF16)
    gext[5:7] = g_coarse.astype(F32).reshape(2, 8, CH)
    coarse_halo(gext, 3)
    gc[0] = g_coarse

    @pl.loop(1, GROUPS)
    def _(i):
        send(gc.at[0], gc.at[i], 4, (g + i) % GROUPS, b)

    ccells = jnp.concatenate([ccells, jnp.zeros((32, CH), F32)], axis=0).astype(BF16)
    ct_send[...] = matmul_nt(sort, ccells).astype(BF16).reshape(4, 32, 128)
    ct_recv[0] = ct_send[share]

    @pl.loop(1, GROUPS)
    def _(i):
        to = (g + i) % GROUPS
        send(ct_send.at[to // 4], ct_recv.at[i], 5, to, b)

    out_v[...] = (act_fine + spread(act_coarse, pool)).reshape(2, 4, 16, CH)
    store = pltpu.make_async_copy(out_v, output, local_sem.at[4])
    store.start()

    coarse_halo_wait(gext, 3)
    gcells = gext[...].reshape(96, CH)
    mixed = jnp.zeros((16, 3 * CH), F32)
    for step in range(9):
        start = (2 - step // 3) * 32 + (2 - step % 3) * 8
        window = gcells[start : start + 16].astype(BF16)
        mixed = mixed + matmul_nt(window, wc_v[step])
    back_coarse = mixed[:, CH : 2 * CH]
    back_coarse = back_coarse + neighbours_along_depth(mixed[:, 0:CH], 8)[1]
    back_coarse = back_coarse + neighbours_along_depth(mixed[:, 2 * CH :], 8)[0]
    g_fine = (cot_v[...].reshape(128, CH) + spread(back_coarse, pool) * 0.125) * slope_fine
    gf[0] = g_fine.astype(BF16)

    @pl.loop(1, GROUPS)
    def _(i):
        send(gf.at[0], gf.at[i], 6, (g + i) % GROUPS, b)

    wait_for(et_recv.at[pl.ds(0, GROUPS - 1)], recv_sem.at[1])
    everyone = et_recv[...].reshape(GROUPS * 32, 384)
    for k in range(PART):
        picked = jnp.dot(everyone, selection(quarter * PART + k, 384, 4, 16), preferred_element_type=F32)
        lf[:, k] = picked.astype(BF16).reshape(GROUPS, 32, 128)
    wait_for(ct_recv.at[pl.ds(0, GROUPS - 1)], recv_sem.at[5])
    everyone = ct_recv[...].reshape(GROUPS * 32, 128)
    for k in range(PART):
        picked = jnp.dot(everyone, selection(quarter * PART + k, 128, 2, 8), preferred_element_type=F32)
        lc[:, k] = picked.astype(BF16).reshape(GROUPS, 32, 128)

    def scatter(acc, rows, sums, total, phase):
        acc[0 : PART * 32] = total
        acc[PART * 32 :] = jnp.zeros((32, CH), F32)
        for brick in range(BRICKS):
            rows[brick] = acc[pl.ds(brick, 8, stride=32), :]
        sums[0] = rows[b]

        @pl.loop(1, BRICKS)
        def _(i):
            to = (b + i) % BRICKS
            send(rows.at[to], sums.at[i], phase, g, to)

    def gather(sums, fin, phase, after):
        wait_for(sums.at[pl.ds(0, BRICKS - 1)], recv_sem.at[phase])
        fin[g] = jnp.sum(sums[...], axis=0)

        @pl.loop(1, GROUPS)
        def _(i):
            send(fin.at[g], fin.at[g], after, (g + i) % GROUPS, b)

    wait_for(gc.at[pl.ds(0, GROUPS - 1)], recv_sem.at[4])
    total = jnp.zeros((PART * 32, CH), F32)
    for member in range(GROUPS):
        grads = jnp.concatenate([gc[member], jnp.zeros((112, CH), BF16)], axis=0)
        total = total + jnp.dot(lc[member].reshape(PART * 32, 128), grads, preferred_element_type=F32)
    scatter(acc_c, rows_c, sum_c, total, 7)

    wait_for(gf.at[pl.ds(0, GROUPS - 1)], recv_sem.at[6])
    total = jnp.zeros((PART * 32, CH), F32)
    for member in range(GROUPS):
        total = total + jnp.dot(lf[member].reshape(PART * 32, 128), gf[member], preferred_element_type=F32)
    scatter(acc_f, rows_f, sum_f, total, 8)

    gather(sum_c, fin_c, 7, 9)
    gather(sum_f, fin_f, 8, 10)

    def place(fin, grad, phase):
        wait_for(fin.at[pl.ds(0, GROUPS - 1)], recv_sem.at[phase])
        for member in range(GROUPS):
            channel, part = member // 4, member % 4
            count = PART if part < 3 else PART - 1
            grad[pl.ds(part * PART * 4 + channel, count, stride=4), :] = fin[member, 0:count]

    place(fin_c, grad_coarse, 9)
    place(fin_f, grad_fine, 10)

    wait_for(et_recv.at[pl.ds(0, GROUPS - 1)], send_sem.at[1])
    wait_for(gc.at[pl.ds(0, GROUPS - 1)], send_sem.at[4])
    wait_for(ct_recv.at[pl.ds(0, GROUPS - 1)], send_sem.at[5])
    wait_for(gf.at[pl.ds(0, GROUPS - 1)], send_sem.at[6])
    wait_for(sum_c.at[pl.ds(0, BRICKS - 1)], send_sem.at[7])
    wait_for(sum_f.at[pl.ds(0, BRICKS - 1)], send_sem.at[8])
    wait_for(fin_c.at[pl.ds(0, GROUPS - 1)], send_sem.at[9])
    wait_for(fin_f.at[pl.ds(0, GROUPS - 1)], send_sem.at[10])
    store.wait()


def body(field, cotangent, w_fine, w_coarse):
    anywhere = pl.BlockSpec(memory_space=pl.ANY)
    vmem = pl.BlockSpec(memory_space=pltpu.VMEM)
    fine = (2, 4, 16, CH)
    output, grad_fine, grad_coarse = pl.pallas_call(
        kernel,
        out_shape=(
            jax.ShapeDtypeStruct(fine, F32),
            jax.ShapeDtypeStruct((27 * 4, CH), F32),
            jax.ShapeDtypeStruct((27 * 4, CH), F32),
        ),
        in_specs=[anywhere] * 4,
        out_specs=(anywhere, vmem, vmem),
        scratch_shapes=[
            pltpu.VMEM(fine, F32),
            pltpu.VMEM(fine, F32),
            pltpu.VMEM(fine, F32),
            pltpu.VMEM((9, 3 * CH, CH), BF16),
            pltpu.VMEM((9, 3 * CH, CH), BF16),
            pltpu.VMEM((4, 6, 16, CH), BF16),
            pltpu.VMEM((4, 6, 16, 3 * CH), BF16),
            pltpu.VMEM((32, CH), F32),
            pltpu.VMEM((12, 8, CH), F32),
            pltpu.VMEM((12, 8, CH), F32),
            pltpu.VMEM((4, 32, 384), BF16),
            pltpu.VMEM((GROUPS, 32, 384), BF16),
            pltpu.VMEM((4, 32, 128), BF16),
            pltpu.VMEM((GROUPS, 32, 128), BF16),
            pltpu.VMEM((GROUPS, PART, 32, 128), BF16),
            pltpu.VMEM((GROUPS, PART, 32, 128), BF16),
            pltpu.VMEM((GROUPS, 128, CH), BF16),
            pltpu.VMEM((GROUPS, 16, CH), BF16),
            pltpu.VMEM((256, CH), F32),
            pltpu.VMEM((256, CH), F32),
            pltpu.VMEM((BRICKS, 8, CH), F32),
            pltpu.VMEM((BRICKS, 8, CH), F32),
            pltpu.VMEM((BRICKS, 8, CH), F32),
            pltpu.VMEM((BRICKS, 8, CH), F32),
            pltpu.VMEM((GROUPS, 8, CH), F32),
            pltpu.VMEM((GROUPS, 8, CH), F32),
            pltpu.SemaphoreType.DMA((5,)),
            pltpu.SemaphoreType.DMA((11,)),
            pltpu.SemaphoreType.DMA((11,)),
        ],
        compiler_params=pltpu.CompilerParams(
            collective_id=0, has_side_effects=True, vmem_limit_bytes=32 * 1024 * 1024
        ),
        cost_estimate=pl.CostEstimate(flops=600_000_000, bytes_accessed=2_500_000, transcendentals=40_000),
        name="unet_levels",
    )(field, cotangent, w_fine.reshape(9, 3 * CH, CH), w_coarse.reshape(9, 3 * CH, CH))
    return output, grad_fine.reshape(27, 4, CH), grad_coarse.reshape(27, 4, CH)


def solution(mesh):
    in_specs = (P("group", "brick", None, None), P("group", "brick", None, None), P(), P())
    out_specs = (P("group", "brick", None, None), P(None, "brick", None), P(None, "brick", None))
    return jax.shard_map(body, mesh=mesh, in_specs=in_specs, out_specs=out_specs, check_vma=False)
```

```python
import jax
import jax.numpy as jnp
from jax import lax
from jax.experimental import pallas as pl
from jax.experimental.pallas import tpu as pltpu
from jax.sharding import PartitionSpec as P

CH = 128
GROUPS = 16
BRICKS = 32
F32 = jnp.float32
BF16 = jnp.bfloat16
PART = 7
FAR_FIRST = (10, 11, 6, 7, 14, 15, 8, 9, 2, 3, 12, 13, 4, 5, 1)


def brick_targets(b):
    half, ring = b // 16, b % 16
    steps = sorted(range(16), key=lambda step: -min(step, 16 - step))
    return [
        (flip, step, ((half + flip) % 2) * 16 + (ring + step) % 16)
        for step in steps
        for flip in (1, 0)
        if flip or step
    ]


def wait_for(ref, sem):
    pltpu.make_async_copy(ref, ref, sem).wait()


def iota(shape, dim):
    return lax.broadcasted_iota(jnp.int32, shape, dim)


def neighbours_along_depth(rows, depth):
    count = rows.shape[0]
    place = iota(rows.shape, 0) & (depth - 1)
    before = jnp.where(place == 0, 0.0, pltpu.roll(rows, 1, 0))
    after = jnp.where(place == depth - 1, 0.0, pltpu.roll(rows, count - 1, 0))
    return before, after


def matmul_nt(a, b):
    return lax.dot_general(a, b, (((1,), (1,)), ((), ())), preferred_element_type=F32)


def pooled(values, pool):
    pool[...] = jnp.sum(values.reshape(2, 2, 2, 16, CH), axis=(0, 2)).reshape(32, CH)
    return pool[pl.ds(0, 16, stride=2), :] + pool[pl.ds(1, 16, stride=2), :]


def spread(values, pool):
    pool[pl.ds(0, 16, stride=2), :] = values
    pool[pl.ds(1, 16, stride=2), :] = values
    wide = jnp.broadcast_to(pool[...].reshape(1, 2, 1, 16, CH), (2, 2, 2, 16, CH))
    return wide.reshape(128, CH)


def selection(offset, rows, size_y, size_z):
    row = iota((rows, 128), 0)
    cell = iota((rows, 128), 1)
    step_x, step_y, step_z = offset // 9, (offset // 3) % 3, offset % 3
    plane = size_y * size_z
    z = cell % size_z + step_z - 1
    y = (cell // size_z) % size_y + step_y
    x = cell // plane + step_x
    source = (x * (size_y + 2) + y) * size_z + z
    inside = (z >= 0) & (z < size_z)
    if size_y == 2:
        inside = inside & (cell < plane)
    hit = inside & (row == source) & (offset < 27)
    return jnp.where(hit, 1.0, 0.0).astype(BF16)


def kernel(
    field, cot, w_fine, w_coarse, output, grad_fine, grad_coarse,
    field_v, cot_v, wf_v, wc_v, ext, ext3, pool, cext, gext,
    et_send, et_recv, ct_send, ct_recv, lf, lc, gf, gc, acc_f, acc_c,
    rows, sums, fin,
    local_sem, send_sem, recv_sem, gf_sem,
):
    g = lax.axis_index("group")
    b = lax.axis_index("brick")
    g_up, g_down = (g + 1) % GROUPS, (g + GROUPS - 1) % GROUPS
    b_up, b_down = (b + 1) % BRICKS, (b + BRICKS - 1) % BRICKS
    share, quarter = g // 4, g % 4
    mates = [g + m - 2 * sum(((g // bit) % 2) * bit for bit in (1, 2, 4, 8) if m & bit) for m in range(GROUPS)]

    loads = [
        pltpu.make_async_copy(src, dst, local_sem.at[i])
        for i, (src, dst) in enumerate(((field, field_v), (cot, cot_v), (w_fine, wf_v), (w_coarse, wc_v)))
    ]
    for load in loads:
        load.start()

    barrier = pltpu.get_barrier_semaphore()

    def greet(group, brick):
        pl.semaphore_signal(barrier, inc=1, device_id=(group, brick), device_id_type=pl.DeviceIdType.MESH)

    for brick in brick_targets(b):
        greet(g, brick[2])
    for group in (g_up, g_down):
        for brick in (b_up, b_down):
            greet(group, brick)
    for m in FAR_FIRST:
        greet(mates[m], b)

    def copy_to(src, dst, send, recv, group, brick):
        return pltpu.make_async_remote_copy(
            src_ref=src,
            dst_ref=dst,
            send_sem=send,
            recv_sem=recv,
            device_id=(group, brick),
            device_id_type=pl.DeviceIdType.MESH,
        )

    def send(src, dst, phase, group, brick):
        copy_to(src, dst, send_sem.at[phase], recv_sem.at[phase], group, brick).start()

    arrivals = (
        ext.at[pl.ds(0, 4), pl.ds(0, 4)],
        et_recv.at[pl.ds(0, 7), 0],
        cext.at[pl.ds(0, 10)],
        gext.at[pl.ds(0, 10)],
        gc.at[pl.ds(0, GROUPS - 1)],
        ct_recv.at[pl.ds(0, GROUPS - 1)],
        et_recv.at[pl.ds(0, 8), 0],
        sums.at[pl.ds(0, BRICKS - 1)],
        fin.at[pl.ds(0, GROUPS - 1)],
    )

    def arrived(phase):
        wait_for(arrivals[phase], recv_sem.at[phase])

    def sent(phase):
        wait_for(arrivals[phase], send_sem.at[phase])

    loads[0].wait()
    ext[1:3, 1:5] = field_v[...].astype(BF16)
    pl.semaphore_wait(barrier, 4 + GROUPS - 1 + BRICKS - 1)

    send(ext.at[1, 1], ext.at[3, 5], 0, g_down, b_down)
    send(ext.at[1, 4], ext.at[3, 0], 0, g_down, b_up)
    send(ext.at[2, 1], ext.at[0, 5], 0, g_up, b_down)
    send(ext.at[2, 4], ext.at[0, 0], 0, g_up, b_up)
    send(ext.at[1, pl.ds(1, 4)], ext.at[3, pl.ds(1, 4)], 0, g_down, b)
    send(ext.at[2, pl.ds(1, 4)], ext.at[0, pl.ds(1, 4)], 0, g_up, b)
    send(ext.at[pl.ds(1, 2), 1], ext.at[pl.ds(1, 2), 5], 0, g, b_down)
    send(ext.at[pl.ds(1, 2), 4], ext.at[pl.ds(1, 2), 0], 0, g, b_up)

    loads[1].wait()
    d_coarse = pooled(cot_v[...].reshape(128, CH), pool)
    order = iota((CH, CH), 0)
    sort = jnp.where(iota((CH, CH), 1) == 4 * (order % 32) + order // 32, 1.0, 0.0).astype(BF16)
    loads[2].wait()
    loads[3].wait()

    arrived(0)

    def clear(outside, part):
        @pl.when(outside)
        def _():
            ext[part] = jnp.zeros(ext.at[part].shape, BF16)

    clear(g == 0, slice(0, 1))
    clear(g == GROUPS - 1, slice(3, 4))
    clear(b == 0, (slice(0, 4), slice(0, 1)))
    clear(b == BRICKS - 1, (slice(0, 4), slice(5, 6)))

    cells = ext[...].reshape(384, CH)
    before, after = neighbours_along_depth(cells.astype(F32), 16)
    ext3[:, :, :, 0:CH] = before.astype(BF16).reshape(4, 6, 16, CH)
    ext3[:, :, :, CH : 2 * CH] = ext[...]
    ext3[:, :, :, 2 * CH :] = after.astype(BF16).reshape(4, 6, 16, CH)

    z_fine = jnp.zeros((128, CH), F32)
    for step in range(9):
        step_x, step_y = step // 3, step % 3
        window = ext3[step_x : step_x + 2, step_y : step_y + 4].reshape(128, 3 * CH)
        z_fine = z_fine + jnp.dot(window, wf_v[step], preferred_element_type=F32)
    sig = jax.nn.sigmoid(z_fine)
    act_fine = z_fine * sig
    slope_fine = sig * (1.0 + z_fine * (1.0 - sig))
    coarse = (pooled(act_fine, pool) * 0.125).astype(BF16).astype(F32)

    def coarse_halo(buf, phase):
        send(buf.at[5], buf.at[11], phase, g_down, b_down)
        send(buf.at[6], buf.at[8], phase, g_down, b_up)
        send(buf.at[5], buf.at[3], phase, g_up, b_down)
        send(buf.at[6], buf.at[0], phase, g_up, b_up)
        send(buf.at[pl.ds(5, 2)], buf.at[pl.ds(9, 2)], phase, g_down, b)
        send(buf.at[pl.ds(5, 2)], buf.at[pl.ds(1, 2)], phase, g_up, b)
        send(buf.at[5], buf.at[7], phase, g, b_down)
        send(buf.at[6], buf.at[4], phase, g, b_up)

    def coarse_halo_wait(buf, phase):
        arrived(phase)

        def clear(outside, rows):
            @pl.when(outside)
            def _():
                for row in rows:
                    buf[row] = jnp.zeros((8, CH), F32)

        clear(g == 0, (0, 1, 2, 3))
        clear(g == GROUPS - 1, (8, 9, 10, 11))
        clear(b == 0, (0, 4, 8))
        clear(b == BRICKS - 1, (3, 7, 11))

    cext[5:7] = coarse.reshape(2, 8, CH)
    coarse_halo(cext, 2)

    et_send[...] = matmul_nt(sort, cells).astype(BF16).reshape(4, 32, 384)
    for m in FAR_FIRST:
        if m % 2 == 0:
            send(et_send.at[mates[m] // 4], et_recv.at[m // 2, 0], 1, mates[m], b)
    send(et_send.at[share], et_recv.at[0, 1], 6, mates[1], b)
    et_recv[0, 0] = et_send[share]

    coarse_halo_wait(cext, 2)

    ccells = cext[...].reshape(96, CH)
    before, after = neighbours_along_depth(ccells, 8)
    wide = jnp.concatenate([before, ccells, after], axis=1)
    z_coarse = jnp.zeros((16, CH), F32)
    for step in range(9):
        start = (step // 3) * 32 + (step % 3) * 8
        window = wide[start : start + 16].astype(BF16)
        z_coarse = z_coarse + jnp.dot(window, wc_v[step], preferred_element_type=F32)
    sig = jax.nn.sigmoid(z_coarse)
    act_coarse = z_coarse * sig
    g_coarse = d_coarse * (sig * (1.0 + z_coarse * (1.0 - sig)))
    g_coarse = g_coarse.astype(BF16)
    gext[5:7] = g_coarse.astype(F32).reshape(2, 8, CH)
    coarse_halo(gext, 3)

    gc[0] = g_coarse
    for m in FAR_FIRST:
        send(gc.at[0], gc.at[m], 4, mates[m], b)
    ccells = jnp.concatenate([ccells, jnp.zeros((32, CH), F32)], axis=0).astype(BF16)
    ct_send[...] = matmul_nt(sort, ccells).astype(BF16).reshape(4, 32, 128)
    for m in FAR_FIRST:
        send(ct_send.at[mates[m] // 4], ct_recv.at[m], 5, mates[m], b)
    ct_recv[0] = ct_send[share]

    output[...] = (act_fine + spread(act_coarse, pool)).reshape(2, 4, 16, CH)

    arrived(1)
    send(et_recv.at[pl.ds(1, 7), 0], et_recv.at[pl.ds(1, 7), 1], 6, mates[1], b)

    coarse_halo_wait(gext, 3)
    gcells = gext[...].reshape(96, CH)
    mixed = jnp.zeros((16, 3 * CH), F32)
    for step in range(9):
        start = (2 - step // 3) * 32 + (2 - step % 3) * 8
        window = gcells[start : start + 16].astype(BF16)
        mixed = mixed + matmul_nt(window, wc_v[step])
    back_coarse = mixed[:, CH : 2 * CH]
    back_coarse = back_coarse + neighbours_along_depth(mixed[:, 0:CH], 8)[1]
    back_coarse = back_coarse + neighbours_along_depth(mixed[:, 2 * CH :], 8)[0]
    g_fine = (cot_v[...].reshape(128, CH) + spread(back_coarse, pool) * 0.125) * slope_fine
    gf[0] = g_fine.astype(BF16)

    def gf_copy(src, dst, m):
        return copy_to(gf.at[src], gf.at[dst], gf_sem.at[GROUPS + dst], gf_sem.at[dst], mates[m], b)

    for m in FAR_FIRST:
        if m % 2 == 0:
            gf_copy(0, m, m).start()
    gf_copy(0, 1, 1).start()

    arrived(6)
    everyone = et_recv[...].reshape(GROUPS * 32, 384)
    for k in range(PART):
        picked = jnp.dot(everyone, selection(quarter * PART + k, 384, 4, 16), preferred_element_type=F32)
        lf[:, k] = picked.astype(BF16).reshape(GROUPS, 32, 128)
    arrived(5)
    everyone = ct_recv[...].reshape(GROUPS * 32, 128)
    for k in range(PART):
        picked = jnp.dot(everyone, selection(quarter * PART + k, 128, 2, 8), preferred_element_type=F32)
        lc[:, k] = picked.astype(BF16).reshape(GROUPS, 32, 128)

    arrived(4)
    total = jnp.zeros((PART * 32, CH), F32)
    for m in range(GROUPS):
        grads = jnp.concatenate([gc[m], jnp.zeros((112, CH), BF16)], axis=0)
        total = total + jnp.dot(lc[m].reshape(PART * 32, 128), grads, preferred_element_type=F32)
    acc_c[0 : PART * 32] = total
    acc_c[PART * 32 :] = jnp.zeros((32, CH), F32)
    acc_f[PART * 32 :] = jnp.zeros((32, CH), F32)

    total = jnp.dot(lf[0].reshape(PART * 32, 128), gf[0], preferred_element_type=F32)

    def take(total, m):
        gf_copy(0, m, m).wait_recv()
        if m % 2 == 0:
            gf_copy(m, m + 1, 1).start()
        return total + jnp.dot(lf[m].reshape(PART * 32, 128), gf[m], preferred_element_type=F32)

    last = 1
    for m in reversed(FAR_FIRST):
        if m % 2 == 0:
            total = take(total, m)
            total = take(total, last)
            last = m + 1
    total = take(total, last)

    acc_f[0 : PART * 32] = total
    for brick in range(BRICKS):
        pair = [acc[pl.ds(brick, 8, stride=32), :] for acc in (acc_f, acc_c)]
        rows[brick] = jnp.concatenate(pair, axis=0).astype(BF16)
    for high, step, brick in brick_targets(b):
        send(rows.at[brick], sums.at[high * 16 + step], 7, g, brick)
    sums[0] = rows[b]
    arrived(7)
    fin[g] = jnp.sum(sums[...].astype(F32), axis=0)
    for m in FAR_FIRST:
        send(fin.at[g], fin.at[g], 8, mates[m], b)

    for phase in range(8):
        sent(phase)
    for m in range(1, GROUPS):
        gf_copy(0, m, m).wait_send()

    arrived(8)
    for member in range(GROUPS):
        channel, part = member // 4, member % 4
        count = PART if part < 3 else PART - 1
        where = pl.ds(part * PART, count)
        grad_fine[where, channel, :] = fin[member, 0:count]
        grad_coarse[where, channel, :] = fin[member, 8 : 8 + count]
    sent(8)


def copy_out(output, grad_fine, grad_coarse, output_to, grad_fine_to, grad_coarse_to, sem):
    copies = [
        pltpu.make_async_copy(src, dst, sem.at[i])
        for i, (src, dst) in enumerate(
            ((output, output_to), (grad_fine, grad_fine_to), (grad_coarse, grad_coarse_to))
        )
    ]
    for copy in copies:
        copy.start()
    for copy in copies:
        copy.wait()


def body(field, cotangent, w_fine, w_coarse):
    anywhere = pl.BlockSpec(memory_space=pl.ANY)
    vmem = pl.BlockSpec(memory_space=pltpu.VMEM)
    fine = (2, 4, 16, CH)
    shapes = (
        jax.ShapeDtypeStruct(fine, F32),
        jax.ShapeDtypeStruct((27, 4, CH), F32),
        jax.ShapeDtypeStruct((27, 4, CH), F32),
    )
    results = pl.pallas_call(
        kernel,
        out_shape=tuple(pltpu.VMEM(shape.shape, shape.dtype) for shape in shapes),
        in_specs=[anywhere] * 4,
        out_specs=(vmem, vmem, vmem),
        scratch_shapes=[
            pltpu.VMEM(fine, F32),
            pltpu.VMEM(fine, F32),
            pltpu.VMEM((9, 3 * CH, CH), BF16),
            pltpu.VMEM((9, 3 * CH, CH), BF16),
            pltpu.VMEM((4, 6, 16, CH), BF16),
            pltpu.VMEM((4, 6, 16, 3 * CH), BF16),
            pltpu.VMEM((32, CH), F32),
            pltpu.VMEM((12, 8, CH), F32),
            pltpu.VMEM((12, 8, CH), F32),
            pltpu.VMEM((4, 32, 384), BF16),
            pltpu.VMEM((8, 2, 32, 384), BF16),
            pltpu.VMEM((4, 32, 128), BF16),
            pltpu.VMEM((GROUPS, 32, 128), BF16),
            pltpu.VMEM((GROUPS, PART, 32, 128), BF16),
            pltpu.VMEM((GROUPS, PART, 32, 128), BF16),
            pltpu.VMEM((GROUPS, 128, CH), BF16),
            pltpu.VMEM((GROUPS, 16, CH), BF16),
            pltpu.VMEM((256, CH), F32),
            pltpu.VMEM((256, CH), F32),
            pltpu.VMEM((BRICKS, 16, CH), BF16),
            pltpu.VMEM((BRICKS, 16, CH), BF16),
            pltpu.VMEM((GROUPS, 16, CH), F32),
            pltpu.SemaphoreType.DMA((4,)),
            pltpu.SemaphoreType.DMA((9,)),
            pltpu.SemaphoreType.DMA((9,)),
            pltpu.SemaphoreType.DMA((2 * GROUPS,)),
        ],
        compiler_params=pltpu.CompilerParams(
            collective_id=0, has_side_effects=True, vmem_limit_bytes=60 * 1024 * 1024
        ),
        cost_estimate=pl.CostEstimate(flops=600_000_000, bytes_accessed=2_500_000, transcendentals=40_000),
        name="unet_levels",
    )(field, cotangent, w_fine.reshape(9, 3 * CH, CH), w_coarse.reshape(9, 3 * CH, CH))
    return pl.pallas_call(
        copy_out,
        out_shape=shapes,
        in_specs=[vmem] * 3,
        out_specs=(anywhere,) * 3,
        scratch_shapes=[pltpu.SemaphoreType.DMA((3,))],
        compiler_params=pltpu.CompilerParams(vmem_limit_bytes=1024 * 1024),
        name="copy_out",
    )(*results)


def solution(mesh):
    in_specs = (P("group", "brick", None, None), P("group", "brick", None, None), P(), P())
    out_specs = (P("group", "brick", None, None), P(None, "brick", None), P(None, "brick", None))
    return jax.shard_map(body, mesh=mesh, in_specs=in_specs, out_specs=out_specs, check_vma=False)
```

```python
import jax
import jax.numpy as jnp
from jax import lax
from jax.experimental import pallas as pl
from jax.experimental.pallas import tpu as pltpu
from jax.sharding import PartitionSpec as P

CH = 128
GROUPS = 16
BRICKS = 32
F32 = jnp.float32
BF16 = jnp.bfloat16
PART = 7
FAR_FIRST = (10, 11, 6, 7, 14, 15, 8, 9, 2, 3, 12, 13, 4, 5, 1)


def brick_targets(b):
    half, ring = b // 16, b % 16
    steps = sorted(range(16), key=lambda step: -min(step, 16 - step))
    return [
        (flip, step, ((half + flip) % 2) * 16 + (ring + step) % 16)
        for step in steps
        for flip in (1, 0)
        if flip or step
    ]


def wait_for(ref, sem):
    pltpu.make_async_copy(ref, ref, sem).wait()


def iota(shape, dim):
    return lax.broadcasted_iota(jnp.int32, shape, dim)


def neighbours_along_depth(rows, depth):
    count = rows.shape[0]
    place = iota(rows.shape, 0) & (depth - 1)
    before = jnp.where(place == 0, 0.0, pltpu.roll(rows, 1, 0))
    after = jnp.where(place == depth - 1, 0.0, pltpu.roll(rows, count - 1, 0))
    return before, after


def matmul_nt(a, b):
    return lax.dot_general(a, b, (((1,), (1,)), ((), ())), preferred_element_type=F32)


def pooled(values, pool):
    pool[...] = jnp.sum(values.reshape(2, 2, 2, 16, CH), axis=(0, 2)).reshape(32, CH)
    return pool[pl.ds(0, 16, stride=2), :] + pool[pl.ds(1, 16, stride=2), :]


def spread(values, pool):
    pool[pl.ds(0, 16, stride=2), :] = values
    pool[pl.ds(1, 16, stride=2), :] = values
    wide = jnp.broadcast_to(pool[...].reshape(1, 2, 1, 16, CH), (2, 2, 2, 16, CH))
    return wide.reshape(128, CH)


def selection(offset, rows, size_y, size_z):
    row = iota((rows, 128), 0)
    cell = iota((rows, 128), 1)
    step_x, step_y, step_z = offset // 9, (offset // 3) % 3, offset % 3
    plane = size_y * size_z
    z = cell % size_z + step_z - 1
    y = (cell // size_z) % size_y + step_y
    x = cell // plane + step_x
    source = (x * (size_y + 2) + y) * size_z + z
    inside = (z >= 0) & (z < size_z)
    if size_y == 2:
        inside = inside & (cell < plane)
    hit = inside & (row == source) & (offset < 27)
    return jnp.where(hit, 1.0, 0.0).astype(BF16)


def kernel(
    field, cot, w_fine, w_coarse, output, grad_fine, grad_coarse,
    field_v, cot_v, wf_v, wc_v, ext, ext3, pool, wide_pool, cext, gext,
    et_send, et_all, cot_all, slope_all, ct_send, ct_all, lf, lc, acc_f, acc_c,
    rows, sums, fin,
    local_sem, send_sem, recv_sem,
):
    g = lax.axis_index("group")
    b = lax.axis_index("brick")
    g_up, g_down = (g + 1) % GROUPS, (g + GROUPS - 1) % GROUPS
    b_up, b_down = (b + 1) % BRICKS, (b + BRICKS - 1) % BRICKS
    share, quarter = g // 4, g % 4
    mates = [g + m - 2 * sum(((g // bit) % 2) * bit for bit in (1, 2, 4, 8) if m & bit) for m in range(GROUPS)]

    loads = [
        pltpu.make_async_copy(src, dst, local_sem.at[i])
        for i, (src, dst) in enumerate(((field, field_v), (cot, cot_v), (w_fine, wf_v), (w_coarse, wc_v)))
    ]
    for load in loads:
        load.start()

    barrier = pltpu.get_barrier_semaphore()

    def greet(group, brick):
        pl.semaphore_signal(barrier, inc=1, device_id=(group, brick), device_id_type=pl.DeviceIdType.MESH)

    for brick in brick_targets(b):
        greet(g, brick[2])
    for group in (g_up, g_down):
        for brick in (b_up, b_down):
            greet(group, brick)
    for m in FAR_FIRST:
        greet(mates[m], b)

    def copy_to(src, dst, send, recv, group, brick):
        return pltpu.make_async_remote_copy(
            src_ref=src,
            dst_ref=dst,
            send_sem=send,
            recv_sem=recv,
            device_id=(group, brick),
            device_id_type=pl.DeviceIdType.MESH,
        )

    def send(src, dst, phase, group, brick):
        copy_to(src, dst, send_sem.at[phase], recv_sem.at[phase], group, brick).start()

    arrivals = (
        ext.at[pl.ds(0, 4), pl.ds(0, 4)],
        cot_all.at[pl.ds(0, 7), 0],
        cext.at[pl.ds(0, 10)],
        slope_all.at[pl.ds(0, 7), 0],
        gext.at[pl.ds(0, 3 * GROUPS - 1)],
        ct_all.at[pl.ds(0, GROUPS - 1)],
        et_all.at[pl.ds(0, 7), 0],
        sums.at[pl.ds(0, BRICKS - 1)],
        fin.at[pl.ds(0, GROUPS - 1)],
        cot_all.at[pl.ds(0, 8), 0],
        slope_all.at[pl.ds(0, 8), 0],
        et_all.at[pl.ds(0, 8), 0],
    )

    def arrived(phase):
        wait_for(arrivals[phase], recv_sem.at[phase])

    def sent(phase):
        wait_for(arrivals[phase], send_sem.at[phase])

    chip, core = g // 2, g % 2

    def spread_out(src_of, buf, phase):
        for m in FAR_FIRST:
            if m % 2 == 0:
                send(src_of(mates[m]), buf.at[chip, core], phase, mates[m], b)

    def relay(buf, phase, after):
        arrived(phase)
        send(buf.at[:, core], buf.at[:, core], after, mates[1], b)

    loads[0].wait()
    ext[1:3, 1:5] = field_v[...].astype(BF16)
    pl.semaphore_wait(barrier, 4 + GROUPS - 1 + BRICKS - 1)

    send(ext.at[1, 1], ext.at[3, 5], 0, g_down, b_down)
    send(ext.at[1, 4], ext.at[3, 0], 0, g_down, b_up)
    send(ext.at[2, 1], ext.at[0, 5], 0, g_up, b_down)
    send(ext.at[2, 4], ext.at[0, 0], 0, g_up, b_up)
    send(ext.at[1, pl.ds(1, 4)], ext.at[3, pl.ds(1, 4)], 0, g_down, b)
    send(ext.at[2, pl.ds(1, 4)], ext.at[0, pl.ds(1, 4)], 0, g_up, b)
    send(ext.at[pl.ds(1, 2), 1], ext.at[pl.ds(1, 2), 5], 0, g, b_down)
    send(ext.at[pl.ds(1, 2), 4], ext.at[pl.ds(1, 2), 0], 0, g, b_up)

    loads[1].wait()
    cot_rows = cot_v[...].reshape(128, CH)
    cot_all[chip, core] = cot_rows.astype(BF16)
    spread_out(lambda mate: cot_all.at[chip, core], cot_all, 1)
    d_coarse = pooled(cot_rows, pool)
    order = iota((CH, CH), 0)
    sort = jnp.where(iota((CH, CH), 1) == 4 * (order % 32) + order // 32, 1.0, 0.0).astype(BF16)
    loads[2].wait()
    loads[3].wait()

    arrived(0)

    def clear(outside, part):
        @pl.when(outside)
        def _():
            ext[part] = jnp.zeros(ext.at[part].shape, BF16)

    clear(g == 0, slice(0, 1))
    clear(g == GROUPS - 1, slice(3, 4))
    clear(b == 0, (slice(0, 4), slice(0, 1)))
    clear(b == BRICKS - 1, (slice(0, 4), slice(5, 6)))

    cells = ext[...].reshape(384, CH)
    before, after = neighbours_along_depth(cells.astype(F32), 16)
    ext3[:, :, :, 0:CH] = before.astype(BF16).reshape(4, 6, 16, CH)
    ext3[:, :, :, CH : 2 * CH] = ext[...]
    ext3[:, :, :, 2 * CH :] = after.astype(BF16).reshape(4, 6, 16, CH)

    z_fine = jnp.zeros((128, CH), F32)
    for step in range(9):
        step_x, step_y = step // 3, step % 3
        window = ext3[step_x : step_x + 2, step_y : step_y + 4].reshape(128, 3 * CH)
        z_fine = z_fine + jnp.dot(window, wf_v[step], preferred_element_type=F32)
    sig = jax.nn.sigmoid(z_fine)
    act_fine = z_fine * sig
    slope_fine = sig * (1.0 + z_fine * (1.0 - sig))
    coarse = (pooled(act_fine, pool) * 0.125).astype(BF16).astype(F32)

    def coarse_halo(buf, phase):
        send(buf.at[5], buf.at[11], phase, g_down, b_down)
        send(buf.at[6], buf.at[8], phase, g_down, b_up)
        send(buf.at[5], buf.at[3], phase, g_up, b_down)
        send(buf.at[6], buf.at[0], phase, g_up, b_up)
        send(buf.at[pl.ds(5, 2)], buf.at[pl.ds(9, 2)], phase, g_down, b)
        send(buf.at[pl.ds(5, 2)], buf.at[pl.ds(1, 2)], phase, g_up, b)
        send(buf.at[5], buf.at[7], phase, g, b_down)
        send(buf.at[6], buf.at[4], phase, g, b_up)

    def coarse_halo_wait(buf, phase):
        arrived(phase)

        def clear(outside, rows):
            @pl.when(outside)
            def _():
                for row in rows:
                    buf[row] = jnp.zeros((8, CH), F32)

        clear(g == 0, (0, 1, 2, 3))
        clear(g == GROUPS - 1, (8, 9, 10, 11))
        clear(b == 0, (0, 4, 8))
        clear(b == BRICKS - 1, (3, 7, 11))

    cext[5:7] = coarse.reshape(2, 8, CH)
    coarse_halo(cext, 2)

    slope_all[chip, core] = slope_fine.astype(BF16)
    spread_out(lambda mate: slope_all.at[chip, core], slope_all, 3)

    et_send[...] = matmul_nt(sort, cells).astype(BF16).reshape(4, 32, 384)
    spread_out(lambda mate: et_send.at[mate // 4], et_all, 6)
    et_all[chip, core] = et_send[share]
    relay(cot_all, 1, 9)

    coarse_halo_wait(cext, 2)

    ccells = cext[...].reshape(96, CH)
    before, after = neighbours_along_depth(ccells, 8)
    wide = jnp.concatenate([before, ccells, after], axis=1)
    z_coarse = jnp.zeros((16, CH), F32)
    for step in range(9):
        start = (step // 3) * 32 + (step % 3) * 8
        window = wide[start : start + 16].astype(BF16)
        z_coarse = z_coarse + jnp.dot(window, wc_v[step], preferred_element_type=F32)
    sig = jax.nn.sigmoid(z_coarse)
    act_coarse = z_coarse * sig
    g_coarse = d_coarse * (sig * (1.0 + z_coarse * (1.0 - sig)))
    g_coarse = g_coarse.astype(BF16)

    own = (g + 1) * 3
    gext[own + 1] = g_coarse
    for m in FAR_FIRST + (0,):
        send(gext.at[own + 1], gext.at[own + 2], 4, mates[m], b_down)
        send(gext.at[own + 1], gext.at[own], 4, mates[m], b_up)
        if m:
            send(gext.at[own + 1], gext.at[own + 1], 4, mates[m], b)
    for row in (0, 1, 2, 51, 52, 53):
        gext[row] = jnp.zeros((16, CH), BF16)

    ccells = jnp.concatenate([ccells, jnp.zeros((32, CH), F32)], axis=0).astype(BF16)
    ct_send[...] = matmul_nt(sort, ccells).astype(BF16).reshape(4, 32, 128)
    for m in FAR_FIRST:
        send(ct_send.at[mates[m] // 4], ct_all.at[g], 5, mates[m], b)
    ct_all[g] = ct_send[share]

    output[...] = (act_fine + spread(act_coarse, pool)).reshape(2, 4, 16, CH)

    relay(slope_all, 3, 10)
    relay(et_all, 6, 11)

    arrived(11)
    everyone = et_all[...].reshape(GROUPS * 32, 384)
    for k in range(0, PART, 2):
        steps = range(k, min(k + 2, PART))
        chosen = [selection(quarter * PART + step, 384, 4, 16) for step in steps]
        picked = jnp.dot(everyone, jnp.concatenate(chosen, axis=1), preferred_element_type=F32)
        picked = picked.astype(BF16).reshape(8, 2, 32, len(chosen) * 128)
        for i, step in enumerate(steps):
            for half in range(2):
                lf[:, step, :, half * 128 : (half + 1) * 128] = picked[:, half, :, i * 128 : (i + 1) * 128]
    arrived(5)
    everyone = ct_all[...].reshape(GROUPS * 32, 128)
    for k in range(0, PART, 2):
        steps = range(k, min(k + 2, PART))
        chosen = [selection(quarter * PART + step, 128, 2, 8) for step in steps]
        picked = jnp.dot(everyone, jnp.concatenate(chosen, axis=1), preferred_element_type=F32)
        picked = picked.astype(BF16).reshape(8, 2, 32, len(chosen) * 128)
        for i, step in enumerate(steps):
            for half in range(2):
                lc[:, step, :, half * 128 : (half + 1) * 128] = picked[:, half, :, i * 128 : (i + 1) * 128]
    arrived(9)
    arrived(10)

    arrived(4)

    def clear_gext(outside, place):
        @pl.when(outside)
        def _():
            for x in range(GROUPS):
                gext[(x + 1) * 3 + place] = jnp.zeros((16, CH), BF16)

    clear_gext(b == 0, 0)
    clear_gext(b == BRICKS - 1, 2)

    gcells = gext[...].astype(F32).reshape(GROUPS + 2, 6, 8, CH)
    mixed = jnp.zeros((GROUPS * 16, 3 * CH), F32)
    for step in range(9):
        step_x, step_y = step // 3, step % 3
        window = gcells[2 - step_x : 18 - step_x, 3 - step_y : 5 - step_y].reshape(GROUPS * 16, CH)
        mixed = mixed + matmul_nt(window.astype(BF16), wc_v[step])
    back_coarse = mixed[:, CH : 2 * CH]
    back_coarse = back_coarse + neighbours_along_depth(mixed[:, 0:CH], 8)[1]
    back_coarse = back_coarse + neighbours_along_depth(mixed[:, 2 * CH :], 8)[0]
    back_coarse = back_coarse * 0.125
    wide_pool[pl.ds(0, GROUPS * 16, stride=2), :] = back_coarse
    wide_pool[pl.ds(1, GROUPS * 16, stride=2), :] = back_coarse
    total = jnp.zeros((PART * 32, CH), F32)
    for pair in range(8):
        back = wide_pool[pair * 64 : (pair + 1) * 64].reshape(2, 1, 2, 1, 16, CH)
        back = jnp.broadcast_to(back, (2, 2, 2, 2, 16, CH)).reshape(256, CH)
        grads = cot_all[pair].reshape(256, CH).astype(F32) + back
        grads = (grads * slope_all[pair].reshape(256, CH).astype(F32)).astype(BF16)
        total = total + jnp.dot(lf[pair].reshape(PART * 32, 256), grads, preferred_element_type=F32)
    acc_f[0 : PART * 32] = total

    total = jnp.zeros((PART * 32, CH), F32)
    empty = jnp.zeros((112, CH), BF16)
    for pair in range(8):
        first, second = (gext[(2 * pair + i + 1) * 3 + 1] for i in range(2))
        grads = jnp.concatenate([first, empty, second, empty], axis=0)
        total = total + jnp.dot(lc[pair].reshape(PART * 32, 256), grads, preferred_element_type=F32)
    acc_c[0 : PART * 32] = total
    acc_c[PART * 32 :] = jnp.zeros((32, CH), F32)
    acc_f[PART * 32 :] = jnp.zeros((32, CH), F32)

    for brick in range(BRICKS):
        pair = [acc[pl.ds(brick, 8, stride=32), :] for acc in (acc_f, acc_c)]
        rows[brick] = jnp.concatenate(pair, axis=0).astype(BF16)
    for high, step, brick in brick_targets(b):
        send(rows.at[brick], sums.at[high * 16 + step], 7, g, brick)
    sums[0] = rows[b]
    arrived(7)
    fin[g] = jnp.sum(sums[...].astype(F32), axis=0)
    for m in FAR_FIRST:
        send(fin.at[g], fin.at[g], 8, mates[m], b)

    for phase in (0, 1, 2, 3, 4, 5, 6, 7, 9, 10, 11):
        sent(phase)

    arrived(8)
    for member in range(GROUPS):
        channel, part = member // 4, member % 4
        count = PART if part < 3 else PART - 1
        where = pl.ds(part * PART, count)
        grad_fine[where, channel, :] = fin[member, 0:count]
        grad_coarse[where, channel, :] = fin[member, 8 : 8 + count]
    sent(8)


def copy_out(output, grad_fine, grad_coarse, output_to, grad_fine_to, grad_coarse_to, sem):
    copies = [
        pltpu.make_async_copy(src, dst, sem.at[i])
        for i, (src, dst) in enumerate(
            ((output, output_to), (grad_fine, grad_fine_to), (grad_coarse, grad_coarse_to))
        )
    ]
    for copy in copies:
        copy.start()
    for copy in copies:
        copy.wait()


def body(field, cotangent, w_fine, w_coarse):
    anywhere = pl.BlockSpec(memory_space=pl.ANY)
    vmem = pl.BlockSpec(memory_space=pltpu.VMEM)
    fine = (2, 4, 16, CH)
    shapes = (
        jax.ShapeDtypeStruct(fine, F32),
        jax.ShapeDtypeStruct((27, 4, CH), F32),
        jax.ShapeDtypeStruct((27, 4, CH), F32),
    )
    results = pl.pallas_call(
        kernel,
        out_shape=tuple(pltpu.VMEM(shape.shape, shape.dtype) for shape in shapes),
        in_specs=[anywhere] * 4,
        out_specs=(vmem, vmem, vmem),
        scratch_shapes=[
            pltpu.VMEM(fine, F32),
            pltpu.VMEM(fine, F32),
            pltpu.VMEM((9, 3 * CH, CH), BF16),
            pltpu.VMEM((9, 3 * CH, CH), BF16),
            pltpu.VMEM((4, 6, 16, CH), BF16),
            pltpu.VMEM((4, 6, 16, 3 * CH), BF16),
            pltpu.VMEM((32, CH), F32),
            pltpu.VMEM((GROUPS * 32, CH), F32),
            pltpu.VMEM((12, 8, CH), F32),
            pltpu.VMEM(((GROUPS + 2) * 3, 16, CH), BF16),
            pltpu.VMEM((4, 32, 384), BF16),
            pltpu.VMEM((8, 2, 32, 384), BF16),
            pltpu.VMEM((8, 2, 128, CH), BF16),
            pltpu.VMEM((8, 2, 128, CH), BF16),
            pltpu.VMEM((4, 32, 128), BF16),
            pltpu.VMEM((GROUPS, 32, 128), BF16),
            pltpu.VMEM((8, PART, 32, 256), BF16),
            pltpu.VMEM((8, PART, 32, 256), BF16),
            pltpu.VMEM((256, CH), F32),
            pltpu.VMEM((256, CH), F32),
            pltpu.VMEM((BRICKS, 16, CH), BF16),
            pltpu.VMEM((BRICKS, 16, CH), BF16),
            pltpu.VMEM((GROUPS, 16, CH), F32),
            pltpu.SemaphoreType.DMA((4,)),
            pltpu.SemaphoreType.DMA((12,)),
            pltpu.SemaphoreType.DMA((12,)),
        ],
        compiler_params=pltpu.CompilerParams(
            collective_id=0, has_side_effects=True, vmem_limit_bytes=60 * 1024 * 1024
        ),
        cost_estimate=pl.CostEstimate(flops=600_000_000, bytes_accessed=2_500_000, transcendentals=40_000),
        name="unet_levels",
    )(field, cotangent, w_fine.reshape(9, 3 * CH, CH), w_coarse.reshape(9, 3 * CH, CH))
    return pl.pallas_call(
        copy_out,
        out_shape=shapes,
        in_specs=[vmem] * 3,
        out_specs=(anywhere,) * 3,
        scratch_shapes=[pltpu.SemaphoreType.DMA((3,))],
        compiler_params=pltpu.CompilerParams(vmem_limit_bytes=1024 * 1024),
        name="copy_out",
    )(*results)


def solution(mesh):
    in_specs = (P("group", "brick", None, None), P("group", "brick", None, None), P(), P())
    out_specs = (P("group", "brick", None, None), P(None, "brick", None), P(None, "brick", None))
    return jax.shard_map(body, mesh=mesh, in_specs=in_specs, out_specs=out_specs, check_vma=False)
```

```python
import jax
import jax.numpy as jnp
from jax import lax
from jax.experimental import pallas as pl
from jax.experimental.pallas import tpu as pltpu
from jax.sharding import PartitionSpec as P

CH = 128
GROUPS = 16
BRICKS = 32
F32 = jnp.float32
BF16 = jnp.bfloat16
PART = 7
FAR_FIRST = (10, 11, 6, 7, 14, 15, 8, 9, 2, 3, 12, 13, 4, 5, 1)


def brick_targets(b):
    half, ring = b // 16, b % 16
    steps = sorted(range(16), key=lambda step: -min(step, 16 - step))
    return [
        (flip, step, ((half + flip) % 2) * 16 + (ring + step) % 16)
        for step in steps
        for flip in (1, 0)
        if flip or step
    ]


def wait_for(ref, sem):
    pltpu.make_async_copy(ref, ref, sem).wait()


def iota(shape, dim):
    return lax.broadcasted_iota(jnp.int32, shape, dim)


def neighbours_along_depth(rows, depth):
    count = rows.shape[0]
    place = iota(rows.shape, 0) & (depth - 1)
    before = jnp.where(place == 0, 0.0, pltpu.roll(rows, 1, 0))
    after = jnp.where(place == depth - 1, 0.0, pltpu.roll(rows, count - 1, 0))
    return before, after


def matmul_nt(a, b):
    return lax.dot_general(a, b, (((1,), (1,)), ((), ())), preferred_element_type=F32)


def pooled(values, pool):
    pool[...] = jnp.sum(values.reshape(2, 2, 2, 16, CH), axis=(0, 2)).reshape(32, CH)
    return pool[pl.ds(0, 16, stride=2), :] + pool[pl.ds(1, 16, stride=2), :]


def spread(values, pool):
    pool[pl.ds(0, 16, stride=2), :] = values
    pool[pl.ds(1, 16, stride=2), :] = values
    wide = jnp.broadcast_to(pool[...].reshape(1, 2, 1, 16, CH), (2, 2, 2, 16, CH))
    return wide.reshape(128, CH)


def selection(offset, rows, size_y, size_z):
    row = iota((rows, 128), 0)
    cell = iota((rows, 128), 1)
    step_x, step_y, step_z = offset // 9, (offset // 3) % 3, offset % 3
    plane = size_y * size_z
    z = cell % size_z + step_z - 1
    y = (cell // size_z) % size_y + step_y
    x = cell // plane + step_x
    source = (x * (size_y + 2) + y) * size_z + z
    inside = (z >= 0) & (z < size_z)
    if size_y == 2:
        inside = inside & (cell < plane)
    hit = inside & (row == source) & (offset < 27)
    return jnp.where(hit, 1.0, 0.0).astype(BF16)


def kernel(
    field, cot, w_fine, w_coarse, output, grad_fine, grad_coarse,
    field_v, cot_v, wf_v, wc_v, ext, ext3, pool, wide_pool, cext, gext,
    et_send, et_all, cot_all, slope_all, ct_send, ct_all, lf, lc, acc_f, acc_c,
    rows, sums, fin,
    local_sem, send_sem, recv_sem, ring_sem,
):
    g = lax.axis_index("group")
    b = lax.axis_index("brick")
    g_up, g_down = (g + 1) % GROUPS, (g + GROUPS - 1) % GROUPS
    b_up, b_down = (b + 1) % BRICKS, (b + BRICKS - 1) % BRICKS
    share, quarter = g // 4, g % 4
    mates = [g + m - 2 * sum(((g // bit) % 2) * bit for bit in (1, 2, 4, 8) if m & bit) for m in range(GROUPS)]

    loads = [
        pltpu.make_async_copy(src, dst, local_sem.at[i])
        for i, (src, dst) in enumerate(((field, field_v), (cot, cot_v), (w_fine, wf_v), (w_coarse, wc_v)))
    ]
    for load in loads:
        load.start()

    barrier = pltpu.get_barrier_semaphore()

    def greet(group, brick):
        pl.semaphore_signal(barrier, inc=1, device_id=(group, brick), device_id_type=pl.DeviceIdType.MESH)

    for group in (g_up, g_down):
        for brick in (b_up, b_down):
            greet(group, brick)
    for m in FAR_FIRST:
        greet(mates[m], b)
    greet(g, b_up)
    greet(g, b_down)

    def tell(stage):
        for brick in ((b + 2**stage) % BRICKS, (b + BRICKS - 2**stage) % BRICKS):
            pl.semaphore_signal(
                ring_sem.at[stage], inc=1, device_id=(g, brick), device_id_type=pl.DeviceIdType.MESH
            )

    def heard(stage):
        pl.semaphore_wait(ring_sem.at[stage], 2)

    def copy_to(src, dst, send, recv, group, brick):
        return pltpu.make_async_remote_copy(
            src_ref=src,
            dst_ref=dst,
            send_sem=send,
            recv_sem=recv,
            device_id=(group, brick),
            device_id_type=pl.DeviceIdType.MESH,
        )

    def send(src, dst, phase, group, brick):
        copy_to(src, dst, send_sem.at[phase], recv_sem.at[phase], group, brick).start()

    arrivals = (
        ext.at[pl.ds(0, 4), pl.ds(0, 4)],
        cot_all.at[pl.ds(0, 7), 0],
        cext.at[pl.ds(0, 10)],
        slope_all.at[pl.ds(0, 7), 0],
        gext.at[pl.ds(0, 3 * GROUPS - 1)],
        ct_all.at[pl.ds(0, GROUPS - 1)],
        et_all.at[pl.ds(0, 7), 0],
        sums.at[pl.ds(0, BRICKS - 1)],
        fin.at[pl.ds(0, GROUPS - 1)],
        cot_all.at[pl.ds(0, 8), 0],
        slope_all.at[pl.ds(0, 8), 0],
        et_all.at[pl.ds(0, 8), 0],
    )

    def arrived(phase):
        wait_for(arrivals[phase], recv_sem.at[phase])

    def sent(phase):
        wait_for(arrivals[phase], send_sem.at[phase])

    chip, core = g // 2, g % 2

    def spread_out(src_of, buf, phase):
        for m in FAR_FIRST:
            if m % 2 == 0:
                send(src_of(mates[m]), buf.at[chip, core], phase, mates[m], b)

    def relay(buf, phase, after):
        arrived(phase)
        send(buf.at[:, core], buf.at[:, core], after, mates[1], b)

    loads[0].wait()
    ext[1:3, 1:5] = field_v[...].astype(BF16)
    pl.semaphore_wait(barrier, 6 + GROUPS - 1)

    send(ext.at[1, 1], ext.at[3, 5], 0, g_down, b_down)
    send(ext.at[1, 4], ext.at[3, 0], 0, g_down, b_up)
    send(ext.at[2, 1], ext.at[0, 5], 0, g_up, b_down)
    send(ext.at[2, 4], ext.at[0, 0], 0, g_up, b_up)
    send(ext.at[1, pl.ds(1, 4)], ext.at[3, pl.ds(1, 4)], 0, g_down, b)
    send(ext.at[2, pl.ds(1, 4)], ext.at[0, pl.ds(1, 4)], 0, g_up, b)
    send(ext.at[pl.ds(1, 2), 1], ext.at[pl.ds(1, 2), 5], 0, g, b_down)
    send(ext.at[pl.ds(1, 2), 4], ext.at[pl.ds(1, 2), 0], 0, g, b_up)

    tell(0)

    loads[1].wait()
    cot_rows = cot_v[...].reshape(128, CH)
    cot_all[chip, core] = cot_rows.astype(BF16)
    spread_out(lambda mate: cot_all.at[chip, core], cot_all, 1)
    d_coarse = pooled(cot_rows, pool)
    order = iota((CH, CH), 0)
    sort = jnp.where(iota((CH, CH), 1) == 4 * (order % 32) + order // 32, 1.0, 0.0).astype(BF16)
    loads[2].wait()
    loads[3].wait()

    heard(0)
    tell(1)
    arrived(0)

    def clear(outside, part):
        @pl.when(outside)
        def _():
            ext[part] = jnp.zeros(ext.at[part].shape, BF16)

    clear(g == 0, slice(0, 1))
    clear(g == GROUPS - 1, slice(3, 4))
    clear(b == 0, (slice(0, 4), slice(0, 1)))
    clear(b == BRICKS - 1, (slice(0, 4), slice(5, 6)))

    cells = ext[...].reshape(384, CH)
    before, after = neighbours_along_depth(cells.astype(F32), 16)
    ext3[:, :, :, 0:CH] = before.astype(BF16).reshape(4, 6, 16, CH)
    ext3[:, :, :, CH : 2 * CH] = ext[...]
    ext3[:, :, :, 2 * CH :] = after.astype(BF16).reshape(4, 6, 16, CH)

    z_fine = jnp.zeros((128, CH), F32)
    for step in range(9):
        step_x, step_y = step // 3, step % 3
        window = ext3[step_x : step_x + 2, step_y : step_y + 4].reshape(128, 3 * CH)
        z_fine = z_fine + jnp.dot(window, wf_v[step], preferred_element_type=F32)
    sig = jax.nn.sigmoid(z_fine)
    act_fine = z_fine * sig
    slope_fine = sig * (1.0 + z_fine * (1.0 - sig))
    coarse = (pooled(act_fine, pool) * 0.125).astype(BF16).astype(F32)

    def coarse_halo(buf, phase):
        send(buf.at[5], buf.at[11], phase, g_down, b_down)
        send(buf.at[6], buf.at[8], phase, g_down, b_up)
        send(buf.at[5], buf.at[3], phase, g_up, b_down)
        send(buf.at[6], buf.at[0], phase, g_up, b_up)
        send(buf.at[pl.ds(5, 2)], buf.at[pl.ds(9, 2)], phase, g_down, b)
        send(buf.at[pl.ds(5, 2)], buf.at[pl.ds(1, 2)], phase, g_up, b)
        send(buf.at[5], buf.at[7], phase, g, b_down)
        send(buf.at[6], buf.at[4], phase, g, b_up)

    def coarse_halo_wait(buf, phase):
        arrived(phase)

        def clear(outside, rows):
            @pl.when(outside)
            def _():
                for row in rows:
                    buf[row] = jnp.zeros((8, CH), F32)

        clear(g == 0, (0, 1, 2, 3))
        clear(g == GROUPS - 1, (8, 9, 10, 11))
        clear(b == 0, (0, 4, 8))
        clear(b == BRICKS - 1, (3, 7, 11))

    cext[5:7] = coarse.reshape(2, 8, CH)
    coarse_halo(cext, 2)

    slope_all[chip, core] = slope_fine.astype(BF16)
    spread_out(lambda mate: slope_all.at[chip, core], slope_all, 3)

    et_send[...] = matmul_nt(sort, cells).astype(BF16).reshape(4, 32, 384)
    spread_out(lambda mate: et_send.at[mate // 4], et_all, 6)
    et_all[chip, core] = et_send[share]
    heard(1)
    tell(2)
    relay(cot_all, 1, 9)
    heard(2)
    tell(3)

    coarse_halo_wait(cext, 2)

    ccells = cext[...].reshape(96, CH)
    before, after = neighbours_along_depth(ccells, 8)
    wide = jnp.concatenate([before, ccells, after], axis=1)
    z_coarse = jnp.zeros((16, CH), F32)
    for step in range(9):
        start = (step // 3) * 32 + (step % 3) * 8
        window = wide[start : start + 16].astype(BF16)
        z_coarse = z_coarse + jnp.dot(window, wc_v[step], preferred_element_type=F32)
    sig = jax.nn.sigmoid(z_coarse)
    act_coarse = z_coarse * sig
    g_coarse = d_coarse * (sig * (1.0 + z_coarse * (1.0 - sig)))
    g_coarse = g_coarse.astype(BF16)

    own = (g + 1) * 3
    gext[own + 1] = g_coarse
    for m in FAR_FIRST + (0,):
        send(gext.at[own + 1], gext.at[own + 2], 4, mates[m], b_down)
        send(gext.at[own + 1], gext.at[own], 4, mates[m], b_up)
        if m:
            send(gext.at[own + 1], gext.at[own + 1], 4, mates[m], b)
    for row in (0, 1, 2, 51, 52, 53):
        gext[row] = jnp.zeros((16, CH), BF16)

    ccells = jnp.concatenate([ccells, jnp.zeros((32, CH), F32)], axis=0).astype(BF16)
    ct_send[...] = matmul_nt(sort, ccells).astype(BF16).reshape(4, 32, 128)
    for m in FAR_FIRST:
        send(ct_send.at[mates[m] // 4], ct_all.at[g], 5, mates[m], b)
    ct_all[g] = ct_send[share]

    output[...] = (act_fine + spread(act_coarse, pool)).reshape(2, 4, 16, CH)

    relay(slope_all, 3, 10)
    relay(et_all, 6, 11)

    arrived(11)
    everyone = et_all[...].reshape(GROUPS * 32, 384)
    for k in range(0, PART, 2):
        steps = range(k, min(k + 2, PART))
        chosen = [selection(quarter * PART + step, 384, 4, 16) for step in steps]
        picked = jnp.dot(everyone, jnp.concatenate(chosen, axis=1), preferred_element_type=F32)
        picked = picked.astype(BF16).reshape(8, 2, 32, len(chosen) * 128)
        for i, step in enumerate(steps):
            for half in range(2):
                lf[:, step, :, half * 128 : (half + 1) * 128] = picked[:, half, :, i * 128 : (i + 1) * 128]
    arrived(5)
    everyone = ct_all[...].reshape(GROUPS * 32, 128)
    for k in range(0, PART, 2):
        steps = range(k, min(k + 2, PART))
        chosen = [selection(quarter * PART + step, 128, 2, 8) for step in steps]
        picked = jnp.dot(everyone, jnp.concatenate(chosen, axis=1), preferred_element_type=F32)
        picked = picked.astype(BF16).reshape(8, 2, 32, len(chosen) * 128)
        for i, step in enumerate(steps):
            for half in range(2):
                lc[:, step, :, half * 128 : (half + 1) * 128] = picked[:, half, :, i * 128 : (i + 1) * 128]
    arrived(9)
    arrived(10)

    arrived(4)

    def clear_gext(outside, place):
        @pl.when(outside)
        def _():
            for x in range(GROUPS):
                gext[(x + 1) * 3 + place] = jnp.zeros((16, CH), BF16)

    clear_gext(b == 0, 0)
    clear_gext(b == BRICKS - 1, 2)

    gcells = gext[...].astype(F32).reshape(GROUPS + 2, 6, 8, CH)
    mixed = jnp.zeros((GROUPS * 16, 3 * CH), F32)
    for step in range(9):
        step_x, step_y = step // 3, step % 3
        window = gcells[2 - step_x : 18 - step_x, 3 - step_y : 5 - step_y].reshape(GROUPS * 16, CH)
        mixed = mixed + matmul_nt(window.astype(BF16), wc_v[step])
    back_coarse = mixed[:, CH : 2 * CH]
    back_coarse = back_coarse + neighbours_along_depth(mixed[:, 0:CH], 8)[1]
    back_coarse = back_coarse + neighbours_along_depth(mixed[:, 2 * CH :], 8)[0]
    back_coarse = back_coarse * 0.125
    wide_pool[pl.ds(0, GROUPS * 16, stride=2), :] = back_coarse
    wide_pool[pl.ds(1, GROUPS * 16, stride=2), :] = back_coarse
    total = jnp.zeros((PART * 32, CH), F32)
    for pair in range(8):
        back = wide_pool[pair * 64 : (pair + 1) * 64].reshape(2, 1, 2, 1, 16, CH)
        back = jnp.broadcast_to(back, (2, 2, 2, 2, 16, CH)).reshape(256, CH)
        grads = cot_all[pair].reshape(256, CH).astype(F32) + back
        grads = (grads * slope_all[pair].reshape(256, CH).astype(F32)).astype(BF16)
        total = total + jnp.dot(lf[pair].reshape(PART * 32, 256), grads, preferred_element_type=F32)
    acc_f[0 : PART * 32] = total

    total = jnp.zeros((PART * 32, CH), F32)
    empty = jnp.zeros((112, CH), BF16)
    for pair in range(8):
        first, second = (gext[(2 * pair + i + 1) * 3 + 1] for i in range(2))
        grads = jnp.concatenate([first, empty, second, empty], axis=0)
        total = total + jnp.dot(lc[pair].reshape(PART * 32, 256), grads, preferred_element_type=F32)
    acc_c[0 : PART * 32] = total
    acc_c[PART * 32 :] = jnp.zeros((32, CH), F32)
    acc_f[PART * 32 :] = jnp.zeros((32, CH), F32)

    for brick in range(BRICKS):
        pair = [acc[pl.ds(brick, 8, stride=32), :] for acc in (acc_f, acc_c)]
        rows[brick] = jnp.concatenate(pair, axis=0).astype(BF16)
    heard(3)
    for high, step, brick in brick_targets(b):
        send(rows.at[brick], sums.at[high * 16 + step], 7, g, brick)
    sums[0] = rows[b]
    arrived(7)
    fin[g] = jnp.sum(sums[...].astype(F32), axis=0)
    for m in FAR_FIRST:
        send(fin.at[g], fin.at[g], 8, mates[m], b)

    for phase in (0, 1, 2, 3, 4, 5, 6, 7, 9, 10, 11):
        sent(phase)

    arrived(8)
    for member in range(GROUPS):
        channel, part = member // 4, member % 4
        count = PART if part < 3 else PART - 1
        where = pl.ds(part * PART, count)
        grad_fine[where, channel, :] = fin[member, 0:count]
        grad_coarse[where, channel, :] = fin[member, 8 : 8 + count]
    sent(8)


def copy_out(output, grad_fine, grad_coarse, output_to, grad_fine_to, grad_coarse_to, sem):
    copies = [
        pltpu.make_async_copy(src, dst, sem.at[i])
        for i, (src, dst) in enumerate(
            ((output, output_to), (grad_fine, grad_fine_to), (grad_coarse, grad_coarse_to))
        )
    ]
    for copy in copies:
        copy.start()
    for copy in copies:
        copy.wait()


def body(field, cotangent, w_fine, w_coarse):
    anywhere = pl.BlockSpec(memory_space=pl.ANY)
    vmem = pl.BlockSpec(memory_space=pltpu.VMEM)
    fine = (2, 4, 16, CH)
    shapes = (
        jax.ShapeDtypeStruct(fine, F32),
        jax.ShapeDtypeStruct((27, 4, CH), F32),
        jax.ShapeDtypeStruct((27, 4, CH), F32),
    )
    results = pl.pallas_call(
        kernel,
        out_shape=tuple(pltpu.VMEM(shape.shape, shape.dtype) for shape in shapes),
        in_specs=[anywhere] * 4,
        out_specs=(vmem, vmem, vmem),
        scratch_shapes=[
            pltpu.VMEM(fine, F32),
            pltpu.VMEM(fine, F32),
            pltpu.VMEM((9, 3 * CH, CH), BF16),
            pltpu.VMEM((9, 3 * CH, CH), BF16),
            pltpu.VMEM((4, 6, 16, CH), BF16),
            pltpu.VMEM((4, 6, 16, 3 * CH), BF16),
            pltpu.VMEM((32, CH), F32),
            pltpu.VMEM((GROUPS * 32, CH), F32),
            pltpu.VMEM((12, 8, CH), F32),
            pltpu.VMEM(((GROUPS + 2) * 3, 16, CH), BF16),
            pltpu.VMEM((4, 32, 384), BF16),
            pltpu.VMEM((8, 2, 32, 384), BF16),
            pltpu.VMEM((8, 2, 128, CH), BF16),
            pltpu.VMEM((8, 2, 128, CH), BF16),
            pltpu.VMEM((4, 32, 128), BF16),
            pltpu.VMEM((GROUPS, 32, 128), BF16),
            pltpu.VMEM((8, PART, 32, 256), BF16),
            pltpu.VMEM((8, PART, 32, 256), BF16),
            pltpu.VMEM((256, CH), F32),
            pltpu.VMEM((256, CH), F32),
            pltpu.VMEM((BRICKS, 16, CH), BF16),
            pltpu.VMEM((BRICKS, 16, CH), BF16),
            pltpu.VMEM((GROUPS, 16, CH), F32),
            pltpu.SemaphoreType.DMA((4,)),
            pltpu.SemaphoreType.DMA((12,)),
            pltpu.SemaphoreType.DMA((12,)),
            pltpu.SemaphoreType.REGULAR((4,)),
        ],
        compiler_params=pltpu.CompilerParams(
            collective_id=0, has_side_effects=True, vmem_limit_bytes=60 * 1024 * 1024
        ),
        cost_estimate=pl.CostEstimate(flops=600_000_000, bytes_accessed=2_500_000, transcendentals=40_000),
        name="unet_levels",
    )(field, cotangent, w_fine.reshape(9, 3 * CH, CH), w_coarse.reshape(9, 3 * CH, CH))
    return pl.pallas_call(
        copy_out,
        out_shape=shapes,
        in_specs=[vmem] * 3,
        out_specs=(anywhere,) * 3,
        scratch_shapes=[pltpu.SemaphoreType.DMA((3,))],
        compiler_params=pltpu.CompilerParams(vmem_limit_bytes=1024 * 1024),
        name="copy_out",
    )(*results)


def solution(mesh):
    in_specs = (P("group", "brick", None, None), P("group", "brick", None, None), P(), P())
    out_specs = (P("group", "brick", None, None), P(None, "brick", None), P(None, "brick", None))
    return jax.shard_map(body, mesh=mesh, in_specs=in_specs, out_specs=out_specs, check_vma=False)
```

```python
import jax
import jax.numpy as jnp
from jax import lax
from jax.experimental import pallas as pl
from jax.experimental.pallas import tpu as pltpu
from jax.sharding import PartitionSpec as P

CH = 128
GROUPS = 16
BRICKS = 32
F32 = jnp.float32
BF16 = jnp.bfloat16
PART = 7
FAR_FIRST = (10, 11, 6, 7, 14, 15, 8, 9, 2, 3, 12, 13, 4, 5, 1)


def brick_targets(b):
    half, ring = b // 16, b % 16
    steps = sorted(range(16), key=lambda step: -min(step, 16 - step))
    return [
        (flip, step, ((half + flip) % 2) * 16 + (ring + step) % 16)
        for step in steps
        for flip in (1, 0)
        if flip or step
    ]


def wait_for(ref, sem):
    pltpu.make_async_copy(ref, ref, sem).wait()


def iota(shape, dim):
    return lax.broadcasted_iota(jnp.int32, shape, dim)


def neighbours_along_depth(rows, depth):
    count = rows.shape[0]
    place = iota(rows.shape, 0) & (depth - 1)
    before = jnp.where(place == 0, 0.0, pltpu.roll(rows, 1, 0))
    after = jnp.where(place == depth - 1, 0.0, pltpu.roll(rows, count - 1, 0))
    return before, after


def matmul_nt(a, b):
    return lax.dot_general(a, b, (((1,), (1,)), ((), ())), preferred_element_type=F32)


def pooled(values, pool):
    pool[...] = jnp.sum(values.reshape(2, 2, 2, 16, CH), axis=(0, 2)).reshape(32, CH)
    return pool[pl.ds(0, 16, stride=2), :] + pool[pl.ds(1, 16, stride=2), :]


def spread(values, pool):
    pool[pl.ds(0, 16, stride=2), :] = values
    pool[pl.ds(1, 16, stride=2), :] = values
    wide = jnp.broadcast_to(pool[...].reshape(1, 2, 1, 16, CH), (2, 2, 2, 16, CH))
    return wide.reshape(128, CH)


def selection(offset):
    row = iota((256, 128), 0)
    cell = iota((256, 128), 1)
    step_y, step_z = (offset // 3) % 3, offset % 3
    z = cell % 16 + step_z - 1
    source = (cell // 64) * 128 + ((cell // 16) % 4 + step_y) * 16 + z
    hit = (z >= 0) & (z < 16) & (row == source)
    return jnp.where(hit, 1.0, 0.0).astype(BF16)


def kernel(
    field, cot, w_fine, w_coarse, output, grad_fine, grad_coarse,
    field_v, cot_v, wf_v, wc_v, ext, ext3, pool, wide_pool, coarse_all, shifted_all, act_all, d_all,
    et_send, et_all, et_rows, cot_all, slope_all, lf, lc, acc_f, acc_c,
    rows, sums, fin,
    local_sem, send_sem, recv_sem, ring_sem,
):
    g = lax.axis_index("group")
    b = lax.axis_index("brick")
    g_up, g_down = (g + 1) % GROUPS, (g + GROUPS - 1) % GROUPS
    b_up, b_down = (b + 1) % BRICKS, (b + BRICKS - 1) % BRICKS
    share, quarter = g // 4, g % 4
    mates = [g + m - 2 * sum(((g // bit) % 2) * bit for bit in (1, 2, 4, 8) if m & bit) for m in range(GROUPS)]

    loads = [
        pltpu.make_async_copy(src, dst, local_sem.at[i])
        for i, (src, dst) in enumerate(((field, field_v), (cot, cot_v), (w_fine, wf_v), (w_coarse, wc_v)))
    ]
    for load in loads:
        load.start()

    barrier = pltpu.get_barrier_semaphore()

    def greet(group, brick):
        pl.semaphore_signal(barrier, inc=1, device_id=(group, brick), device_id_type=pl.DeviceIdType.MESH)

    for m in FAR_FIRST:
        for brick in (b_up, b_down, b):
            greet(mates[m], brick)
    for step in (4, 3, 2, 1):
        greet(g, (b + step) % BRICKS)
        greet(g, (b + BRICKS - step) % BRICKS)

    def tell(stage):
        for step in (4 * 2**stage, BRICKS - 4 * 2**stage):
            pl.semaphore_signal(
                ring_sem.at[stage], inc=1, device_id=(g, (b + step) % BRICKS), device_id_type=pl.DeviceIdType.MESH
            )

    def heard(stage):
        pl.semaphore_wait(ring_sem.at[stage], 2)

    def copy_to(src, dst, send, recv, group, brick):
        return pltpu.make_async_remote_copy(
            src_ref=src,
            dst_ref=dst,
            send_sem=send,
            recv_sem=recv,
            device_id=(group, brick),
            device_id_type=pl.DeviceIdType.MESH,
        )

    def send(src, dst, phase, group, brick):
        copy_to(src, dst, send_sem.at[phase], recv_sem.at[phase], group, brick).start()

    arrivals = (
        ext.at[pl.ds(0, 4), pl.ds(0, 4)],
        cot_all.at[pl.ds(0, 7), 0],
        wide_pool.at[pl.ds(0, 30 * 8)],
        slope_all.at[pl.ds(0, 7), 0],
        coarse_all.at[pl.ds(0, 3 * GROUPS - 1)],
        d_all.at[pl.ds(0, 8), 0],
        et_all.at[pl.ds(0, 7), 0],
        sums.at[pl.ds(0, BRICKS - 1)],
        fin.at[pl.ds(0, GROUPS - 1)],
        cot_all.at[pl.ds(0, 8), 0],
        slope_all.at[pl.ds(0, 8), 0],
        et_all.at[pl.ds(0, 8), 0],
    )

    def arrived(phase):
        wait_for(arrivals[phase], recv_sem.at[phase])

    def sent(phase):
        wait_for(arrivals[phase], send_sem.at[phase])

    chip, core = g // 2, g % 2

    def spread_out(src_of, buf, phase):
        for m in FAR_FIRST:
            if m % 2 == 0:
                send(src_of(mates[m]), buf.at[chip, core], phase, mates[m], b)

    def relay(buf, phase, after):
        arrived(phase)
        send(buf.at[:, core], buf.at[:, core], after, mates[1], b)

    loads[0].wait()
    ext[1:3, 1:5] = field_v[...].astype(BF16)
    pl.semaphore_wait(barrier, 3 * (GROUPS - 1) + 8)

    send(ext.at[1, 1], ext.at[3, 5], 0, g_down, b_down)
    send(ext.at[1, 4], ext.at[3, 0], 0, g_down, b_up)
    send(ext.at[2, 1], ext.at[0, 5], 0, g_up, b_down)
    send(ext.at[2, 4], ext.at[0, 0], 0, g_up, b_up)
    send(ext.at[1, pl.ds(1, 4)], ext.at[3, pl.ds(1, 4)], 0, g_down, b)
    send(ext.at[2, pl.ds(1, 4)], ext.at[0, pl.ds(1, 4)], 0, g_up, b)
    send(ext.at[pl.ds(1, 2), 1], ext.at[pl.ds(1, 2), 5], 0, g, b_down)
    send(ext.at[pl.ds(1, 2), 4], ext.at[pl.ds(1, 2), 0], 0, g, b_up)

    tell(0)

    loads[1].wait()
    cot_rows = cot_v[...].reshape(128, CH)
    cot_all[chip, core] = cot_rows.astype(BF16)
    spread_out(lambda mate: cot_all.at[chip, core], cot_all, 1)
    d_all[chip, core, 1:3] = pooled(cot_rows, pool).reshape(2, 8, CH)
    for m in FAR_FIRST + (0,):
        if m % 2 == 0:
            send(d_all.at[chip, core, 1], d_all.at[chip, core, 3], 2, mates[m], b_down)
            send(d_all.at[chip, core, 2], d_all.at[chip, core, 0], 2, mates[m], b_up)
            if m:
                send(d_all.at[chip, core, pl.ds(1, 2)], d_all.at[chip, core, pl.ds(1, 2)], 2, mates[m], b)
    for row in (0, 1, 2, 51, 52, 53):
        coarse_all[row] = jnp.zeros((16, CH), BF16)
    order = iota((CH, CH), 0)
    sort = jnp.where(iota((CH, CH), 1) == 4 * (order % 32) + order // 32, 1.0, 0.0).astype(BF16)
    loads[2].wait()
    loads[3].wait()

    arrived(0)

    def clear(outside, part):
        @pl.when(outside)
        def _():
            ext[part] = jnp.zeros(ext.at[part].shape, BF16)

    clear(g == 0, slice(0, 1))
    clear(g == GROUPS - 1, slice(3, 4))
    clear(b == 0, (slice(0, 4), slice(0, 1)))
    clear(b == BRICKS - 1, (slice(0, 4), slice(5, 6)))

    cells = ext[1:3].reshape(2, 96, CH)
    cells = jnp.concatenate([cells, jnp.zeros((2, 32, CH), BF16)], axis=1).reshape(256, CH)
    cells = matmul_nt(sort, cells).astype(BF16).reshape(4, 32, 256)
    for x in range(2):
        et_send[:, x] = cells[:, :, x * 128 : (x + 1) * 128]
    spread_out(lambda mate: et_send.at[mate // 4], et_all, 6)
    et_all[chip, core] = et_send[share]

    cells = ext[...].reshape(384, CH)
    before, after = neighbours_along_depth(cells.astype(F32), 16)
    ext3[:, :, :, 0:CH] = before.astype(BF16).reshape(4, 6, 16, CH)
    ext3[:, :, :, CH : 2 * CH] = ext[...]
    ext3[:, :, :, 2 * CH :] = after.astype(BF16).reshape(4, 6, 16, CH)

    z_fine = jnp.zeros((128, CH), F32)
    for step in range(9):
        step_x, step_y = step // 3, step % 3
        window = ext3[step_x : step_x + 2, step_y : step_y + 4].reshape(128, 3 * CH)
        z_fine = z_fine + jnp.dot(window, wf_v[step], preferred_element_type=F32)
    sig = jax.nn.sigmoid(z_fine)
    act_fine = z_fine * sig
    slope_fine = sig * (1.0 + z_fine * (1.0 - sig))
    coarse = (pooled(act_fine, pool) * 0.125).astype(BF16)

    own = (g + 1) * 3
    coarse_all[own + 1] = coarse
    for m in FAR_FIRST + (0,):
        send(coarse_all.at[own + 1], coarse_all.at[own + 2], 4, mates[m], b_down)
        send(coarse_all.at[own + 1], coarse_all.at[own], 4, mates[m], b_up)
        if m:
            send(coarse_all.at[own + 1], coarse_all.at[own + 1], 4, mates[m], b)

    slope_all[chip, core] = slope_fine.astype(BF16)
    spread_out(lambda mate: slope_all.at[chip, core], slope_all, 3)

    heard(0)
    tell(1)
    relay(cot_all, 1, 9)
    relay(d_all, 2, 5)
    relay(et_all, 6, 11)
    relay(slope_all, 3, 10)

    def offset_of(step):
        return quarter * PART + step - (quarter // 3 if step == PART - 1 else 0)

    arrived(11)
    et_rows[0] = jnp.zeros((32, 128), BF16)
    et_rows[2 * GROUPS + 1] = jnp.zeros((32, 128), BF16)
    et_rows[1 : 2 * GROUPS + 1] = et_all[...].reshape(2 * GROUPS, 32, 128)
    for step in range(PART):
        offset = offset_of(step)
        pairs = et_rows[pl.ds(offset // 9, 2 * GROUPS)].reshape(GROUPS, 2, 32, 128)
        pairs = jnp.concatenate([pairs[:, 0], pairs[:, 1]], axis=2).reshape(GROUPS * 32, 256)
        picked = jnp.dot(pairs, selection(offset), preferred_element_type=F32)
        picked = picked.astype(BF16).reshape(8, 2, 32, 128)
        for half in range(2):
            lf[:, step, :, half * 128 : (half + 1) * 128] = picked[:, half]
    arrived(9)
    arrived(5)
    arrived(10)
    arrived(4)

    def clear_sides(outside, place):
        @pl.when(outside)
        def _():
            for x in range(GROUPS):
                coarse_all[(x + 1) * 3 + place] = jnp.zeros((16, CH), BF16)

    clear_sides(b == 0, 0)
    clear_sides(b == BRICKS - 1, 2)

    ccells = coarse_all[...].astype(F32).reshape((GROUPS + 2) * 48, CH)
    before, after = neighbours_along_depth(ccells, 8)
    for step_z, shifted in enumerate((before, ccells, after)):
        shifted = shifted.reshape(GROUPS + 2, 6, 8, CH)
        for y in range(5):
            shifted_all[step_z, :, y] = shifted[:, y : y + 2].reshape(GROUPS + 2, 16, CH).astype(BF16)
    z_coarse = jnp.zeros((GROUPS * 32, CH), F32)
    for step in range(9):
        step_x, step_y = step // 3, step % 3
        window = [
            jnp.concatenate(
                [shifted_all[step_z, step_x : step_x + GROUPS, step_y + y][:, None] for y in (0, 2)], axis=1
            ).reshape(GROUPS * 32, CH)
            for step_z in range(3)
        ]
        window = jnp.concatenate(window, axis=1)
        z_coarse = z_coarse + jnp.dot(window, wc_v[step], preferred_element_type=F32)
    sig = jax.nn.sigmoid(z_coarse)
    act_all[...] = (z_coarse * sig).reshape(GROUPS, 32, CH)
    d_coarse = d_all[...].reshape(GROUPS * 32, CH)
    row = iota((GROUPS * 32, CH), 0) % 32
    outside = ((row < 8) & (b == 0)) | ((row >= 24) & (b == BRICKS - 1))
    d_coarse = jnp.where(outside, 0.0, d_coarse)
    g_coarse = d_coarse * (sig * (1.0 + z_coarse * (1.0 - sig)))
    g_coarse = g_coarse.astype(BF16).astype(F32).reshape(GROUPS, 4, 8, CH)

    empty = jnp.zeros((1, 4, 8, CH), F32)
    gcells = jnp.concatenate([empty, g_coarse, empty], axis=0)
    mixed = jnp.zeros((GROUPS * 16, 3 * CH), F32)
    for step in range(9):
        step_x, step_y = step // 3, step % 3
        window = gcells[2 - step_x : 18 - step_x, 2 - step_y : 4 - step_y].reshape(GROUPS * 16, CH)
        mixed = mixed + matmul_nt(window.astype(BF16), wc_v[step])
    back_coarse = mixed[:, CH : 2 * CH]
    back_coarse = back_coarse + neighbours_along_depth(mixed[:, 0:CH], 8)[1]
    back_coarse = back_coarse + neighbours_along_depth(mixed[:, 2 * CH :], 8)[0]
    back_coarse = back_coarse * 0.125
    wide_pool[pl.ds(0, GROUPS * 16, stride=2), :] = back_coarse
    wide_pool[pl.ds(1, GROUPS * 16, stride=2), :] = back_coarse
    total = jnp.zeros((PART * 32, CH), F32)
    for pair in range(8):
        back = wide_pool[pair * 64 : (pair + 1) * 64].reshape(2, 1, 2, 1, 16, CH)
        back = jnp.broadcast_to(back, (2, 2, 2, 2, 16, CH)).reshape(256, CH)
        grads = cot_all[pair].reshape(256, CH).astype(F32) + back
        grads = (grads * slope_all[pair].reshape(256, CH).astype(F32)).astype(BF16)
        total = total + jnp.dot(lf[pair].reshape(PART * 32, 256), grads, preferred_element_type=F32)
    acc_f[0 : PART * 32] = total

    row = iota((32, CH), 0)
    own_class = jnp.where(iota((32, CH), 1) == 4 * row + share, 1.0, 0.0).astype(BF16)
    for step in range(PART):
        offset = offset_of(step)
        step_x, step_y, step_z = offset // 9, (offset // 3) % 3, offset % 3
        window = shifted_all[step_z, pl.ds(step_x, GROUPS), step_y + 1].reshape(GROUPS * 16, CH)
        lc[step] = matmul_nt(own_class, window).astype(BF16)
    grads = g_coarse[:, 1:3].reshape(GROUPS * 16, CH).astype(BF16)
    acc_c[0 : PART * 32] = jnp.dot(lc[...].reshape(PART * 32, 256), grads, preferred_element_type=F32)
    acc_c[PART * 32 :] = jnp.zeros((32, CH), F32)
    acc_f[PART * 32 :] = jnp.zeros((32, CH), F32)

    for brick in range(BRICKS):
        pair = [acc[pl.ds(brick, 8, stride=32), :] for acc in (acc_f, acc_c)]
        rows[brick] = jnp.concatenate(pair, axis=0).astype(BF16)
    heard(1)
    for high, step, brick in brick_targets(b):
        send(rows.at[brick], sums.at[high * 16 + step], 7, g, brick)
    sums[0] = rows[b]
    output[...] = (act_fine + spread(act_all[g, 8:24], pool)).reshape(2, 4, 16, CH)
    arrived(7)
    fin[g] = jnp.sum(sums[...].astype(F32), axis=0)
    for m in FAR_FIRST:
        send(fin.at[g], fin.at[g], 8, mates[m], b)

    for phase in (0, 1, 2, 3, 4, 5, 6, 7, 9, 10, 11):
        sent(phase)

    arrived(8)
    for member in range(GROUPS):
        channel, part = member // 4, member % 4
        count = PART if part < 3 else PART - 1
        where = pl.ds(part * PART, count)
        grad_fine[where, channel, :] = fin[member, 0:count]
        grad_coarse[where, channel, :] = fin[member, 8 : 8 + count]
    sent(8)


def copy_out(output, grad_fine, grad_coarse, output_to, grad_fine_to, grad_coarse_to, sem):
    copies = [
        pltpu.make_async_copy(src, dst, sem.at[i])
        for i, (src, dst) in enumerate(
            ((output, output_to), (grad_fine, grad_fine_to), (grad_coarse, grad_coarse_to))
        )
    ]
    for copy in copies:
        copy.start()
    for copy in copies:
        copy.wait()


def body(field, cotangent, w_fine, w_coarse):
    anywhere = pl.BlockSpec(memory_space=pl.ANY)
    vmem = pl.BlockSpec(memory_space=pltpu.VMEM)
    fine = (2, 4, 16, CH)
    shapes = (
        jax.ShapeDtypeStruct(fine, F32),
        jax.ShapeDtypeStruct((27, 4, CH), F32),
        jax.ShapeDtypeStruct((27, 4, CH), F32),
    )
    results = pl.pallas_call(
        kernel,
        out_shape=tuple(pltpu.VMEM(shape.shape, shape.dtype) for shape in shapes),
        in_specs=[anywhere] * 4,
        out_specs=(vmem, vmem, vmem),
        scratch_shapes=[
            pltpu.VMEM(fine, F32),
            pltpu.VMEM(fine, F32),
            pltpu.VMEM((9, 3 * CH, CH), BF16),
            pltpu.VMEM((9, 3 * CH, CH), BF16),
            pltpu.VMEM((4, 6, 16, CH), BF16),
            pltpu.VMEM((4, 6, 16, 3 * CH), BF16),
            pltpu.VMEM((32, CH), F32),
            pltpu.VMEM((GROUPS * 32, CH), F32),
            pltpu.VMEM(((GROUPS + 2) * 3, 16, CH), BF16),
            pltpu.VMEM((3, GROUPS + 2, 5, 16, CH), BF16),
            pltpu.VMEM((GROUPS, 32, CH), F32),
            pltpu.VMEM((8, 2, 4, 8, CH), F32),
            pltpu.VMEM((4, 2, 32, 128), BF16),
            pltpu.VMEM((8, 2, 2, 32, 128), BF16),
            pltpu.VMEM((2 * GROUPS + 2, 32, 128), BF16),
            pltpu.VMEM((8, 2, 128, CH), BF16),
            pltpu.VMEM((8, 2, 128, CH), BF16),
            pltpu.VMEM((8, PART, 32, 256), BF16),
            pltpu.VMEM((PART, 32, 256), BF16),
            pltpu.VMEM((256, CH), F32),
            pltpu.VMEM((256, CH), F32),
            pltpu.VMEM((BRICKS, 16, CH), BF16),
            pltpu.VMEM((BRICKS, 16, CH), BF16),
            pltpu.VMEM((GROUPS, 16, CH), F32),
            pltpu.SemaphoreType.DMA((4,)),
            pltpu.SemaphoreType.DMA((12,)),
            pltpu.SemaphoreType.DMA((12,)),
            pltpu.SemaphoreType.REGULAR((2,)),
        ],
        compiler_params=pltpu.CompilerParams(
            collective_id=0, has_side_effects=True, vmem_limit_bytes=60 * 1024 * 1024
        ),
        cost_estimate=pl.CostEstimate(flops=600_000_000, bytes_accessed=2_500_000, transcendentals=40_000),
        name="unet_levels",
    )(field, cotangent, w_fine.reshape(9, 3 * CH, CH), w_coarse.reshape(9, 3 * CH, CH))
    return pl.pallas_call(
        copy_out,
        out_shape=shapes,
        in_specs=[vmem] * 3,
        out_specs=(anywhere,) * 3,
        scratch_shapes=[pltpu.SemaphoreType.DMA((3,))],
        compiler_params=pltpu.CompilerParams(vmem_limit_bytes=1024 * 1024),
        name="copy_out",
    )(*results)


def solution(mesh):
    in_specs = (P("group", "brick", None, None), P("group", "brick", None, None), P(), P())
    out_specs = (P("group", "brick", None, None), P(None, "brick", None), P(None, "brick", None))
    return jax.shard_map(body, mesh=mesh, in_specs=in_specs, out_specs=out_specs, check_vma=False)
```

```python
import jax
import jax.numpy as jnp
from jax import lax
from jax.experimental import pallas as pl
from jax.experimental.pallas import tpu as pltpu
from jax.sharding import PartitionSpec as P

CH = 128
GROUPS = 16
BRICKS = 32
F32 = jnp.float32
BF16 = jnp.bfloat16
PART = 7
FAR_FIRST = (10, 11, 6, 7, 14, 15, 8, 9, 2, 3, 12, 13, 4, 5, 1)


def brick_targets(b):
    half, ring = b // 16, b % 16
    steps = sorted(range(16), key=lambda step: -min(step, 16 - step))
    return [
        (flip, step, ((half + flip) % 2) * 16 + (ring + step) % 16)
        for step in steps
        for flip in (1, 0)
        if flip or step
    ]


def wait_for(ref, sem):
    pltpu.make_async_copy(ref, ref, sem).wait()


def iota(shape, dim):
    return lax.broadcasted_iota(jnp.int32, shape, dim)


def neighbours_along_depth(rows, depth):
    count = rows.shape[0]
    place = iota(rows.shape, 0) & (depth - 1)
    before = jnp.where(place == 0, 0.0, pltpu.roll(rows, 1, 0))
    after = jnp.where(place == depth - 1, 0.0, pltpu.roll(rows, count - 1, 0))
    return before, after


def matmul_nt(a, b):
    return lax.dot_general(a, b, (((1,), (1,)), ((), ())), preferred_element_type=F32)


def pooled(values, pool):
    pool[...] = jnp.sum(values.reshape(2, 2, 2, 16, CH), axis=(0, 2)).reshape(32, CH)
    return pool[pl.ds(0, 16, stride=2), :] + pool[pl.ds(1, 16, stride=2), :]


def spread(values, pool):
    pool[pl.ds(0, 16, stride=2), :] = values
    pool[pl.ds(1, 16, stride=2), :] = values
    wide = jnp.broadcast_to(pool[...].reshape(1, 2, 1, 16, CH), (2, 2, 2, 16, CH))
    return wide.reshape(128, CH)


def selection(offset):
    row = iota((384, 128), 0)
    cell = iota((384, 128), 1)
    step_x, step_y, step_z = offset // 9, (offset // 3) % 3, offset % 3
    z = cell % 16 + step_z - 1
    source = (cell // 64 + step_x) * 96 + ((cell // 16) % 4 + step_y) * 16 + z
    hit = (z >= 0) & (z < 16) & (row == source)
    return jnp.where(hit, 1.0, 0.0).astype(BF16)


def kernel(
    field, cot, w_fine, w_coarse, output, grad_fine, grad_coarse,
    field_v, cot_v, wf_v, wc_v, ext, ext3, pool, wide_pool, coarse_all, shifted_all, act_all, d_all, g_pairs,
    et_send, et_all, chosen, cot_all, slope_all, lf, lc, both, swapped, acc_f, acc_c,
    rows, sums, fin,
    local_sem, send_sem, recv_sem, ring_sem,
):
    g = lax.axis_index("group")
    b = lax.axis_index("brick")
    g_up, g_down = (g + 1) % GROUPS, (g + GROUPS - 1) % GROUPS
    b_up, b_down = (b + 1) % BRICKS, (b + BRICKS - 1) % BRICKS
    share, quarter = g // 4, g % 4
    mates = [g + m - 2 * sum(((g // bit) % 2) * bit for bit in (1, 2, 4, 8) if m & bit) for m in range(GROUPS)]

    loads = [
        pltpu.make_async_copy(src, dst, local_sem.at[i])
        for i, (src, dst) in enumerate(((field, field_v), (cot, cot_v), (w_fine, wf_v), (w_coarse, wc_v)))
    ]
    for load in loads:
        load.start()

    barrier = pltpu.get_barrier_semaphore()

    def greet(group, brick):
        pl.semaphore_signal(barrier, inc=1, device_id=(group, brick), device_id_type=pl.DeviceIdType.MESH)

    for m in FAR_FIRST:
        for brick in (b_up, b_down, b):
            greet(mates[m], brick)
    for step in (4, 3, 2, 1):
        greet(g, (b + step) % BRICKS)
        greet(g, (b + BRICKS - step) % BRICKS)

    def tell(stage):
        for step in (4 * 2**stage, BRICKS - 4 * 2**stage):
            pl.semaphore_signal(
                ring_sem.at[stage], inc=1, device_id=(g, (b + step) % BRICKS), device_id_type=pl.DeviceIdType.MESH
            )

    def heard(stage):
        pl.semaphore_wait(ring_sem.at[stage], 2)

    def copy_to(src, dst, send, recv, group, brick):
        return pltpu.make_async_remote_copy(
            src_ref=src,
            dst_ref=dst,
            send_sem=send,
            recv_sem=recv,
            device_id=(group, brick),
            device_id_type=pl.DeviceIdType.MESH,
        )

    def send(src, dst, phase, group, brick):
        copy_to(src, dst, send_sem.at[phase], recv_sem.at[phase], group, brick).start()

    arrivals = (
        ext.at[pl.ds(0, 4), pl.ds(0, 4)],
        cot_all.at[pl.ds(0, 7)],
        wide_pool.at[pl.ds(0, 30 * 8)],
        slope_all.at[pl.ds(0, 7)],
        coarse_all.at[pl.ds(0, 3 * GROUPS - 1)],
        d_all.at[pl.ds(0, 8), 0],
        et_all.at[pl.ds(0, 7)],
        sums.at[pl.ds(0, BRICKS - 1)],
        fin.at[pl.ds(0, GROUPS - 1)],
        swapped.at[pl.ds(0, PART * 32)],
    )

    def arrived(phase):
        wait_for(arrivals[phase], recv_sem.at[phase])

    def sent(phase):
        wait_for(arrivals[phase], send_sem.at[phase])

    chip, core = g // 2, g % 2

    def spread_out(src_of, buf, phase):
        for m in FAR_FIRST:
            if m % 2 == 0:
                send(src_of(mates[m]), buf.at[chip], phase, mates[m], b)

    loads[0].wait()
    ext[1:3, 1:5] = field_v[...].astype(BF16)
    pl.semaphore_wait(barrier, 3 * (GROUPS - 1) + 8)

    send(ext.at[1, 1], ext.at[3, 5], 0, g_down, b_down)
    send(ext.at[1, 4], ext.at[3, 0], 0, g_down, b_up)
    send(ext.at[2, 1], ext.at[0, 5], 0, g_up, b_down)
    send(ext.at[2, 4], ext.at[0, 0], 0, g_up, b_up)
    send(ext.at[1, pl.ds(1, 4)], ext.at[3, pl.ds(1, 4)], 0, g_down, b)
    send(ext.at[2, pl.ds(1, 4)], ext.at[0, pl.ds(1, 4)], 0, g_up, b)
    send(ext.at[pl.ds(1, 2), 1], ext.at[pl.ds(1, 2), 5], 0, g, b_down)
    send(ext.at[pl.ds(1, 2), 4], ext.at[pl.ds(1, 2), 0], 0, g, b_up)

    tell(0)

    loads[1].wait()
    cot_rows = cot_v[...].reshape(128, CH)
    cot_all[chip] = cot_rows.astype(BF16)
    spread_out(lambda mate: cot_all.at[chip], cot_all, 1)
    d_all[chip, core, 1:3] = pooled(cot_rows, pool).reshape(2, 8, CH)
    for m in FAR_FIRST + (0,):
        if m % 2 == 0:
            send(d_all.at[chip, core, 1], d_all.at[chip, core, 3], 2, mates[m], b_down)
            send(d_all.at[chip, core, 2], d_all.at[chip, core, 0], 2, mates[m], b_up)
            if m:
                send(d_all.at[chip, core, pl.ds(1, 2)], d_all.at[chip, core, pl.ds(1, 2)], 2, mates[m], b)
    for row in (0, 1, 2, 51, 52, 53):
        coarse_all[row] = jnp.zeros((16, CH), BF16)
    order = iota((CH, CH), 0)
    sort = jnp.where(iota((CH, CH), 1) == 4 * (order % 32) + order // 32, 1.0, 0.0).astype(BF16)
    def offset_of(step):
        return quarter * PART + step - (quarter // 3 if step == PART - 1 else 0)

    half = quarter // 2
    for step in range(0, 2 * PART, 2):
        offset = half * 2 * PART + step
        later = offset + 1 - (half if step + 1 == 2 * PART - 1 else 0)
        chosen[step // 2, :, 0:128] = selection(offset)
        chosen[step // 2, :, 128:256] = selection(later)
    loads[2].wait()
    loads[3].wait()

    arrived(0)

    def clear(outside, part):
        @pl.when(outside)
        def _():
            ext[part] = jnp.zeros(ext.at[part].shape, BF16)

    clear(g == 0, slice(0, 1))
    clear(g == GROUPS - 1, slice(3, 4))
    clear(b == 0, (slice(0, 4), slice(0, 1)))
    clear(b == BRICKS - 1, (slice(0, 4), slice(5, 6)))

    cells = ext[...].reshape(384, CH)
    et_send[...] = matmul_nt(sort, cells).astype(BF16).reshape(4, 32, 384)
    spread_out(lambda mate: et_send.at[mate // 4], et_all, 6)
    et_all[chip] = et_send[share]

    before, after = neighbours_along_depth(cells.astype(F32), 16)
    ext3[:, :, :, 0:CH] = before.astype(BF16).reshape(4, 6, 16, CH)
    ext3[:, :, :, CH : 2 * CH] = ext[...]
    ext3[:, :, :, 2 * CH :] = after.astype(BF16).reshape(4, 6, 16, CH)

    z_fine = jnp.zeros((128, CH), F32)
    for step in range(9):
        step_x, step_y = step // 3, step % 3
        window = ext3[step_x : step_x + 2, step_y : step_y + 4].reshape(128, 3 * CH)
        z_fine = z_fine + jnp.dot(window, wf_v[step], preferred_element_type=F32)
    sig = jax.nn.sigmoid(z_fine)
    act_fine = z_fine * sig
    slope_fine = sig * (1.0 + z_fine * (1.0 - sig))
    coarse = (pooled(act_fine, pool) * 0.125).astype(BF16)

    own = (g + 1) * 3
    coarse_all[own + 1] = coarse
    for m in FAR_FIRST + (0,):
        send(coarse_all.at[own + 1], coarse_all.at[own + 2], 4, mates[m], b_down)
        send(coarse_all.at[own + 1], coarse_all.at[own], 4, mates[m], b_up)
        if m:
            send(coarse_all.at[own + 1], coarse_all.at[own + 1], 4, mates[m], b)

    slope_all[chip] = slope_fine.astype(BF16)
    spread_out(lambda mate: slope_all.at[chip], slope_all, 3)

    heard(0)
    tell(1)
    arrived(2)
    send(d_all.at[:, core], d_all.at[:, core], 5, mates[1], b)

    arrived(6)
    everyone = et_all[...].reshape(8 * 32, 384)
    for step in range(0, 2 * PART, 2):
        picked = jnp.dot(everyone, chosen[step // 2], preferred_element_type=F32).astype(BF16).reshape(4, 2, 32, 256)
        for i in range(2):
            for member in range(2):
                lf[:, step + i, :, member * 128 : (member + 1) * 128] = picked[:, member, :, i * 128 : (i + 1) * 128]
    arrived(1)
    arrived(5)
    arrived(4)

    def clear_sides(outside, place):
        @pl.when(outside)
        def _():
            for x in range(GROUPS):
                coarse_all[(x + 1) * 3 + place] = jnp.zeros((16, CH), BF16)

    clear_sides(b == 0, 0)
    clear_sides(b == BRICKS - 1, 2)

    ccells = coarse_all[...].astype(F32).reshape((GROUPS + 2) * 48, CH)
    before, after = neighbours_along_depth(ccells, 8)
    for step_z, shifted in enumerate((before, ccells, after)):
        shifted = shifted.reshape(GROUPS + 2, 6, 8, CH)
        for y in range(5):
            shifted_all[step_z, :, y] = shifted[:, y : y + 2].reshape(GROUPS + 2, 16, CH).astype(BF16)
    z_coarse = jnp.zeros((GROUPS * 32, CH), F32)
    for step in range(9):
        step_x, step_y = step // 3, step % 3
        window = [
            jnp.concatenate(
                [shifted_all[step_z, step_x : step_x + GROUPS, step_y + y][:, None] for y in (0, 2)], axis=1
            ).reshape(GROUPS * 32, CH)
            for step_z in range(3)
        ]
        window = jnp.concatenate(window, axis=1)
        z_coarse = z_coarse + jnp.dot(window, wc_v[step], preferred_element_type=F32)
    sig = jax.nn.sigmoid(z_coarse)
    act_all[...] = (z_coarse * sig).reshape(GROUPS, 32, CH)
    d_coarse = d_all[...].reshape(GROUPS * 32, CH)
    row = iota((GROUPS * 32, CH), 0) % 32
    outside = ((row < 8) & (b == 0)) | ((row >= 24) & (b == BRICKS - 1))
    d_coarse = jnp.where(outside, 0.0, d_coarse)
    g_coarse = d_coarse * (sig * (1.0 + z_coarse * (1.0 - sig)))
    g_coarse = g_coarse.astype(BF16).astype(F32).reshape(GROUPS, 4, 8, CH)
    g_pairs[0] = jnp.zeros((3, 16, CH), BF16)
    g_pairs[GROUPS + 1] = jnp.zeros((3, 16, CH), BF16)
    for y in range(3):
        g_pairs[1 : GROUPS + 1, y] = g_coarse[:, y : y + 2].reshape(GROUPS, 16, CH).astype(BF16)

    mixed = jnp.zeros((8 * 16, 3 * CH), F32)
    for step in range(9):
        step_x, step_y = step // 3, step % 3
        window = jnp.concatenate([g_pairs[2 * member + core + 2 - step_x, 2 - step_y] for member in range(8)], axis=0)
        mixed = mixed + matmul_nt(window, wc_v[step])
    back_coarse = mixed[:, CH : 2 * CH]
    back_coarse = back_coarse + neighbours_along_depth(mixed[:, 0:CH], 8)[1]
    back_coarse = back_coarse + neighbours_along_depth(mixed[:, 2 * CH :], 8)[0]
    back_coarse = back_coarse * 0.125
    wide_pool[pl.ds(0, 8 * 16, stride=2), :] = back_coarse
    wide_pool[pl.ds(1, 8 * 16, stride=2), :] = back_coarse
    arrived(3)
    total = jnp.zeros((2 * PART * 32, CH), F32)
    for pair in range(4):
        grads = []
        for member in (2 * pair, 2 * pair + 1):
            back = wide_pool[member * 32 : (member + 1) * 32].reshape(1, 2, 1, 16, CH)
            back = jnp.broadcast_to(back, (2, 2, 2, 16, CH)).reshape(128, CH)
            fine = cot_all[member].astype(F32) + back
            grads.append((fine * slope_all[member].astype(F32)).astype(BF16))
        grads = jnp.concatenate(grads, axis=0)
        total = total + jnp.dot(lf[pair].reshape(2 * PART * 32, 256), grads, preferred_element_type=F32)
    both[...] = total.reshape(2, PART * 32, CH)
    send(both.at[1 - core], swapped, 9, mates[1], b)

    row = iota((32, CH), 0)
    own_class = jnp.where(iota((32, CH), 1) == 4 * row + share, 1.0, 0.0).astype(BF16)
    for step in range(PART):
        offset = offset_of(step)
        step_x, step_y, step_z = offset // 9, (offset // 3) % 3, offset % 3
        window = shifted_all[step_z, pl.ds(step_x, GROUPS), step_y + 1].reshape(GROUPS * 16, CH)
        lc[step] = matmul_nt(own_class, window).astype(BF16)
    grads = g_pairs[1 : GROUPS + 1, 1].reshape(GROUPS * 16, CH)
    acc_c[0 : PART * 32] = jnp.dot(lc[...].reshape(PART * 32, 256), grads, preferred_element_type=F32)
    arrived(9)
    acc_f[0 : PART * 32] = both[core] + swapped[...]
    acc_c[PART * 32 :] = jnp.zeros((32, CH), F32)
    acc_f[PART * 32 :] = jnp.zeros((32, CH), F32)

    for brick in range(BRICKS):
        pair = [acc[pl.ds(brick, 8, stride=32), :] for acc in (acc_f, acc_c)]
        rows[brick] = jnp.concatenate(pair, axis=0).astype(BF16)
    heard(1)
    for high, step, brick in brick_targets(b):
        send(rows.at[brick], sums.at[high * 16 + step], 7, g, brick)
    sums[0] = rows[b]
    output[...] = (act_fine + spread(act_all[g, 8:24], pool)).reshape(2, 4, 16, CH)
    arrived(7)
    fin[g] = jnp.sum(sums[...].astype(F32), axis=0)
    for m in FAR_FIRST:
        send(fin.at[g], fin.at[g], 8, mates[m], b)

    for phase in (0, 1, 2, 3, 4, 5, 6, 7, 9):
        sent(phase)

    arrived(8)
    for member in range(GROUPS):
        channel, part = member // 4, member % 4
        count = PART if part < 3 else PART - 1
        where = pl.ds(part * PART, count)
        grad_fine[where, channel, :] = fin[member, 0:count]
        grad_coarse[where, channel, :] = fin[member, 8 : 8 + count]
    sent(8)


def copy_out(output, grad_fine, grad_coarse, output_to, grad_fine_to, grad_coarse_to, sem):
    copies = [
        pltpu.make_async_copy(src, dst, sem.at[i])
        for i, (src, dst) in enumerate(
            ((output, output_to), (grad_fine, grad_fine_to), (grad_coarse, grad_coarse_to))
        )
    ]
    for copy in copies:
        copy.start()
    for copy in copies:
        copy.wait()


def body(field, cotangent, w_fine, w_coarse):
    anywhere = pl.BlockSpec(memory_space=pl.ANY)
    vmem = pl.BlockSpec(memory_space=pltpu.VMEM)
    fine = (2, 4, 16, CH)
    shapes = (
        jax.ShapeDtypeStruct(fine, F32),
        jax.ShapeDtypeStruct((27, 4, CH), F32),
        jax.ShapeDtypeStruct((27, 4, CH), F32),
    )
    results = pl.pallas_call(
        kernel,
        out_shape=tuple(pltpu.VMEM(shape.shape, shape.dtype) for shape in shapes),
        in_specs=[anywhere] * 4,
        out_specs=(vmem, vmem, vmem),
        scratch_shapes=[
            pltpu.VMEM(fine, F32),
            pltpu.VMEM(fine, F32),
            pltpu.VMEM((9, 3 * CH, CH), BF16),
            pltpu.VMEM((9, 3 * CH, CH), BF16),
            pltpu.VMEM((4, 6, 16, CH), BF16),
            pltpu.VMEM((4, 6, 16, 3 * CH), BF16),
            pltpu.VMEM((32, CH), F32),
            pltpu.VMEM((8 * 32, CH), F32),
            pltpu.VMEM(((GROUPS + 2) * 3, 16, CH), BF16),
            pltpu.VMEM((3, GROUPS + 2, 5, 16, CH), BF16),
            pltpu.VMEM((GROUPS, 32, CH), F32),
            pltpu.VMEM((8, 2, 4, 8, CH), F32),
            pltpu.VMEM((GROUPS + 2, 3, 16, CH), BF16),
            pltpu.VMEM((4, 32, 384), BF16),
            pltpu.VMEM((8, 32, 384), BF16),
            pltpu.VMEM((PART, 384, 256), BF16),
            pltpu.VMEM((8, 128, CH), BF16),
            pltpu.VMEM((8, 128, CH), BF16),
            pltpu.VMEM((4, 2 * PART, 32, 256), BF16),
            pltpu.VMEM((PART, 32, 256), BF16),
            pltpu.VMEM((2, PART * 32, CH), F32),
            pltpu.VMEM((PART * 32, CH), F32),
            pltpu.VMEM((256, CH), F32),
            pltpu.VMEM((256, CH), F32),
            pltpu.VMEM((BRICKS, 16, CH), BF16),
            pltpu.VMEM((BRICKS, 16, CH), BF16),
            pltpu.VMEM((GROUPS, 16, CH), F32),
            pltpu.SemaphoreType.DMA((4,)),
            pltpu.SemaphoreType.DMA((10,)),
            pltpu.SemaphoreType.DMA((10,)),
            pltpu.SemaphoreType.REGULAR((2,)),
        ],
        compiler_params=pltpu.CompilerParams(
            collective_id=0, has_side_effects=True, vmem_limit_bytes=60 * 1024 * 1024
        ),
        cost_estimate=pl.CostEstimate(flops=600_000_000, bytes_accessed=2_500_000, transcendentals=40_000),
        name="unet_levels",
    )(field, cotangent, w_fine.reshape(9, 3 * CH, CH), w_coarse.reshape(9, 3 * CH, CH))
    return pl.pallas_call(
        copy_out,
        out_shape=shapes,
        in_specs=[vmem] * 3,
        out_specs=(anywhere,) * 3,
        scratch_shapes=[pltpu.SemaphoreType.DMA((3,))],
        compiler_params=pltpu.CompilerParams(vmem_limit_bytes=1024 * 1024),
        name="copy_out",
    )(*results)


def solution(mesh):
    in_specs = (P("group", "brick", None, None), P("group", "brick", None, None), P(), P())
    out_specs = (P("group", "brick", None, None), P(None, "brick", None), P(None, "brick", None))
    return jax.shard_map(body, mesh=mesh, in_specs=in_specs, out_specs=out_specs, check_vma=False)
```

```python
import jax
import jax.numpy as jnp
from jax import lax
from jax.experimental import pallas as pl
from jax.experimental.pallas import tpu as pltpu
from jax.sharding import PartitionSpec as P

CH = 128
GROUPS = 16
BRICKS = 32
F32 = jnp.float32
BF16 = jnp.bfloat16
PART = 7
FAR_FIRST = (10, 11, 6, 7, 14, 15, 8, 9, 2, 3, 12, 13, 4, 5, 1)


def brick_targets(b):
    half, ring = b // 16, b % 16
    steps = sorted(range(16), key=lambda step: -min(step, 16 - step))
    return [
        (flip, step, ((half + flip) % 2) * 16 + (ring + step) % 16)
        for step in steps
        for flip in (1, 0)
        if flip or step
    ]


def wait_for(ref, sem):
    pltpu.make_async_copy(ref, ref, sem).wait()


def iota(shape, dim):
    return lax.broadcasted_iota(jnp.int32, shape, dim)


def neighbours_along_depth(rows, depth):
    count = rows.shape[0]
    place = iota(rows.shape, 0) & (depth - 1)
    before = jnp.where(place == 0, 0.0, pltpu.roll(rows, 1, 0))
    after = jnp.where(place == depth - 1, 0.0, pltpu.roll(rows, count - 1, 0))
    return before, after


def matmul_nt(a, b):
    return lax.dot_general(a, b, (((1,), (1,)), ((), ())), preferred_element_type=F32)


def pooled(values, pool):
    pool[...] = jnp.sum(values.reshape(2, 2, 2, 16, CH), axis=(0, 2)).reshape(32, CH)
    return pool[pl.ds(0, 16, stride=2), :] + pool[pl.ds(1, 16, stride=2), :]


def spread(values, pool):
    pool[pl.ds(0, 16, stride=2), :] = values
    pool[pl.ds(1, 16, stride=2), :] = values
    wide = jnp.broadcast_to(pool[...].reshape(1, 2, 1, 16, CH), (2, 2, 2, 16, CH))
    return wide.reshape(128, CH)


def selection(offset):
    row = iota((384, 128), 0)
    cell = iota((384, 128), 1)
    z = cell % 16 + offset % 3 - 1
    y = (cell // 16) % 4 + (offset // 3) % 3
    x = cell // 64 + offset // 9
    own = ((x - 1) * 4 + y - 1) * 16
    side = 320 + (x - 1) * 32 + jnp.where(y == 5, 16, 0)
    source = jnp.where((y == 0) | (y == 5), side, own)
    source = jnp.where(x == 0, 128 + y * 16, jnp.where(x == 3, 224 + y * 16, source))
    hit = (z >= 0) & (z < 16) & (row == source + z)
    return jnp.where(hit, 1.0, 0.0).astype(BF16)


def kernel(
    field, cot, w_fine, w_coarse, output, grad_fine, grad_coarse,
    field_v, cot_v, wf_v, wc_v, ext, ext3, pool, wide_pool, coarse_all, shifted_all, act_all, d_all, g_pairs,
    own_send, own_all, rim_send, rim_all, chosen, cot_all, slope_all, lf, lc, both, swapped, acc_f, acc_c,
    rows, sums, fin,
    local_sem, send_sem, recv_sem, ring_sem,
):
    g = lax.axis_index("group")
    b = lax.axis_index("brick")
    g_up, g_down = (g + 1) % GROUPS, (g + GROUPS - 1) % GROUPS
    b_up, b_down = (b + 1) % BRICKS, (b + BRICKS - 1) % BRICKS
    share, quarter = g // 4, g % 4
    mates = [g + m - 2 * sum(((g // bit) % 2) * bit for bit in (1, 2, 4, 8) if m & bit) for m in range(GROUPS)]

    loads = [
        pltpu.make_async_copy(src, dst, local_sem.at[i])
        for i, (src, dst) in enumerate(((field, field_v), (cot, cot_v), (w_fine, wf_v), (w_coarse, wc_v)))
    ]
    for load in loads:
        load.start()

    barrier = pltpu.get_barrier_semaphore()

    def greet(group, brick):
        pl.semaphore_signal(barrier, inc=1, device_id=(group, brick), device_id_type=pl.DeviceIdType.MESH)

    for m in FAR_FIRST:
        for brick in (b_up, b_down, b):
            greet(mates[m], brick)
    for step in (4, 3, 2, 1):
        greet(g, (b + step) % BRICKS)
        greet(g, (b + BRICKS - step) % BRICKS)

    def tell(stage):
        for step in (4 * 2**stage, BRICKS - 4 * 2**stage):
            pl.semaphore_signal(
                ring_sem.at[stage], inc=1, device_id=(g, (b + step) % BRICKS), device_id_type=pl.DeviceIdType.MESH
            )

    def heard(stage):
        pl.semaphore_wait(ring_sem.at[stage], 2)

    def copy_to(src, dst, send, recv, group, brick):
        return pltpu.make_async_remote_copy(
            src_ref=src,
            dst_ref=dst,
            send_sem=send,
            recv_sem=recv,
            device_id=(group, brick),
            device_id_type=pl.DeviceIdType.MESH,
        )

    def send(src, dst, phase, group, brick):
        copy_to(src, dst, send_sem.at[phase], recv_sem.at[phase], group, brick).start()

    arrivals = (
        ext.at[pl.ds(0, 4), pl.ds(0, 4)],
        cot_all.at[pl.ds(0, 7)],
        wide_pool.at[pl.ds(0, 30 * 8)],
        slope_all.at[pl.ds(0, 7)],
        coarse_all.at[pl.ds(0, 3 * GROUPS - 1)],
        d_all.at[pl.ds(0, 8), 0],
        rim_all.at[pl.ds(0, 7)],
        sums.at[pl.ds(0, BRICKS - 1)],
        fin.at[pl.ds(0, GROUPS - 1)],
        swapped.at[pl.ds(0, PART * 32)],
        own_all.at[pl.ds(0, 7)],
    )

    def arrived(phase):
        wait_for(arrivals[phase], recv_sem.at[phase])

    def sent(phase):
        wait_for(arrivals[phase], send_sem.at[phase])

    chip, core = g // 2, g % 2

    def spread_out(src_of, buf, phase):
        for m in FAR_FIRST:
            if m % 2 == 0:
                send(src_of(mates[m]), buf.at[chip], phase, mates[m], b)

    loads[0].wait()
    ext[1:3, 1:5] = field_v[...].astype(BF16)
    pl.semaphore_wait(barrier, 3 * (GROUPS - 1) + 8)

    send(ext.at[1, 1], ext.at[3, 5], 0, g_down, b_down)
    send(ext.at[1, 4], ext.at[3, 0], 0, g_down, b_up)
    send(ext.at[2, 1], ext.at[0, 5], 0, g_up, b_down)
    send(ext.at[2, 4], ext.at[0, 0], 0, g_up, b_up)
    send(ext.at[1, pl.ds(1, 4)], ext.at[3, pl.ds(1, 4)], 0, g_down, b)
    send(ext.at[2, pl.ds(1, 4)], ext.at[0, pl.ds(1, 4)], 0, g_up, b)
    send(ext.at[pl.ds(1, 2), 1], ext.at[pl.ds(1, 2), 5], 0, g, b_down)
    send(ext.at[pl.ds(1, 2), 4], ext.at[pl.ds(1, 2), 0], 0, g, b_up)

    tell(0)

    loads[1].wait()
    cot_rows = cot_v[...].reshape(128, CH)
    cot_all[chip] = cot_rows.astype(BF16)
    spread_out(lambda mate: cot_all.at[chip], cot_all, 1)
    d_all[chip, core, 1:3] = pooled(cot_rows, pool).reshape(2, 8, CH)
    for m in FAR_FIRST + (0,):
        if m % 2 == 0:
            send(d_all.at[chip, core, 1], d_all.at[chip, core, 3], 2, mates[m], b_down)
            send(d_all.at[chip, core, 2], d_all.at[chip, core, 0], 2, mates[m], b_up)
            if m:
                send(d_all.at[chip, core, pl.ds(1, 2)], d_all.at[chip, core, pl.ds(1, 2)], 2, mates[m], b)
    for row in (0, 1, 2, 51, 52, 53):
        coarse_all[row] = jnp.zeros((16, CH), BF16)
    order = iota((CH, CH), 0)
    sort = jnp.where(iota((CH, CH), 1) == 4 * (order % 32) + order // 32, 1.0, 0.0).astype(BF16)
    own_send[...] = matmul_nt(sort, ext[1:3, 1:5].reshape(128, CH)).astype(BF16).reshape(4, 32, 128)
    spread_out(lambda mate: own_send.at[mate // 4], own_all, 10)
    own_all[chip] = own_send[share]

    def offset_of(step):
        return quarter * PART + step - (quarter // 3 if step == PART - 1 else 0)

    half = quarter // 2
    for step in range(0, 2 * PART, 2):
        offset = half * 2 * PART + step
        later = offset + 1 - (half if step + 1 == 2 * PART - 1 else 0)
        chosen[step // 2, :, 0:128] = selection(offset)
        chosen[step // 2, :, 128:256] = selection(later)
    loads[2].wait()
    loads[3].wait()

    arrived(0)

    def clear(outside, part):
        @pl.when(outside)
        def _():
            ext[part] = jnp.zeros(ext.at[part].shape, BF16)

    clear(g == 0, slice(0, 1))
    clear(g == GROUPS - 1, slice(3, 4))
    clear(b == 0, (slice(0, 4), slice(0, 1)))
    clear(b == BRICKS - 1, (slice(0, 4), slice(5, 6)))

    cells = ext[...].reshape(384, CH)
    rim = [ext[0].reshape(96, CH), ext[3].reshape(96, CH), ext[1, 0], ext[1, 5], ext[2, 0], ext[2, 5]]
    rim_send[...] = matmul_nt(sort, jnp.concatenate(rim, axis=0)).astype(BF16).reshape(4, 32, 256)
    spread_out(lambda mate: rim_send.at[mate // 4], rim_all, 6)
    rim_all[chip] = rim_send[share]

    before, after = neighbours_along_depth(cells.astype(F32), 16)
    ext3[:, :, :, 0:CH] = before.astype(BF16).reshape(4, 6, 16, CH)
    ext3[:, :, :, CH : 2 * CH] = ext[...]
    ext3[:, :, :, 2 * CH :] = after.astype(BF16).reshape(4, 6, 16, CH)

    z_fine = jnp.zeros((128, CH), F32)
    for step in range(9):
        step_x, step_y = step // 3, step % 3
        window = ext3[step_x : step_x + 2, step_y : step_y + 4].reshape(128, 3 * CH)
        z_fine = z_fine + jnp.dot(window, wf_v[step], preferred_element_type=F32)
    sig = jax.nn.sigmoid(z_fine)
    act_fine = z_fine * sig
    slope_fine = sig * (1.0 + z_fine * (1.0 - sig))
    coarse = (pooled(act_fine, pool) * 0.125).astype(BF16)

    own = (g + 1) * 3
    coarse_all[own + 1] = coarse
    for m in FAR_FIRST + (0,):
        send(coarse_all.at[own + 1], coarse_all.at[own + 2], 4, mates[m], b_down)
        send(coarse_all.at[own + 1], coarse_all.at[own], 4, mates[m], b_up)
        if m:
            send(coarse_all.at[own + 1], coarse_all.at[own + 1], 4, mates[m], b)

    slope_all[chip] = slope_fine.astype(BF16)
    spread_out(lambda mate: slope_all.at[chip], slope_all, 3)

    heard(0)
    tell(1)
    arrived(2)
    send(d_all.at[:, core], d_all.at[:, core], 5, mates[1], b)

    arrived(10)
    arrived(6)
    everyone = jnp.concatenate([own_all[...], rim_all[...]], axis=2).reshape(8 * 32, 384)
    for step in range(0, 2 * PART, 2):
        picked = jnp.dot(everyone, chosen[step // 2], preferred_element_type=F32).astype(BF16).reshape(4, 2, 32, 256)
        for i in range(2):
            for member in range(2):
                lf[:, step + i, :, member * 128 : (member + 1) * 128] = picked[:, member, :, i * 128 : (i + 1) * 128]
    arrived(1)
    arrived(5)
    arrived(4)

    def clear_sides(outside, place):
        @pl.when(outside)
        def _():
            for x in range(GROUPS):
                coarse_all[(x + 1) * 3 + place] = jnp.zeros((16, CH), BF16)

    clear_sides(b == 0, 0)
    clear_sides(b == BRICKS - 1, 2)

    ccells = coarse_all[...].astype(F32).reshape((GROUPS + 2) * 48, CH)
    before, after = neighbours_along_depth(ccells, 8)
    for step_z, shifted in enumerate((before, ccells, after)):
        shifted = shifted.reshape(GROUPS + 2, 6, 8, CH)
        for y in range(5):
            shifted_all[step_z, :, y] = shifted[:, y : y + 2].reshape(GROUPS + 2, 16, CH).astype(BF16)
    z_coarse = jnp.zeros((GROUPS * 32, CH), F32)
    for step in range(9):
        step_x, step_y = step // 3, step % 3
        window = [
            jnp.concatenate(
                [shifted_all[step_z, step_x : step_x + GROUPS, step_y + y][:, None] for y in (0, 2)], axis=1
            ).reshape(GROUPS * 32, CH)
            for step_z in range(3)
        ]
        window = jnp.concatenate(window, axis=1)
        z_coarse = z_coarse + jnp.dot(window, wc_v[step], preferred_element_type=F32)
    sig = jax.nn.sigmoid(z_coarse)
    act_all[...] = (z_coarse * sig).reshape(GROUPS, 32, CH)
    d_coarse = d_all[...].reshape(GROUPS * 32, CH)
    row = iota((GROUPS * 32, CH), 0) % 32
    outside = ((row < 8) & (b == 0)) | ((row >= 24) & (b == BRICKS - 1))
    d_coarse = jnp.where(outside, 0.0, d_coarse)
    g_coarse = d_coarse * (sig * (1.0 + z_coarse * (1.0 - sig)))
    g_coarse = g_coarse.astype(BF16).astype(F32).reshape(GROUPS, 4, 8, CH)
    g_pairs[0] = jnp.zeros((3, 16, CH), BF16)
    g_pairs[GROUPS + 1] = jnp.zeros((3, 16, CH), BF16)
    for y in range(3):
        g_pairs[1 : GROUPS + 1, y] = g_coarse[:, y : y + 2].reshape(GROUPS, 16, CH).astype(BF16)

    mixed = jnp.zeros((8 * 16, 3 * CH), F32)
    for step in range(9):
        step_x, step_y = step // 3, step % 3
        window = jnp.concatenate([g_pairs[2 * member + core + 2 - step_x, 2 - step_y] for member in range(8)], axis=0)
        mixed = mixed + matmul_nt(window, wc_v[step])
    back_coarse = mixed[:, CH : 2 * CH]
    back_coarse = back_coarse + neighbours_along_depth(mixed[:, 0:CH], 8)[1]
    back_coarse = back_coarse + neighbours_along_depth(mixed[:, 2 * CH :], 8)[0]
    back_coarse = back_coarse * 0.125
    wide_pool[pl.ds(0, 8 * 16, stride=2), :] = back_coarse
    wide_pool[pl.ds(1, 8 * 16, stride=2), :] = back_coarse
    arrived(3)
    total = jnp.zeros((2 * PART * 32, CH), F32)
    for pair in range(4):
        grads = []
        for member in (2 * pair, 2 * pair + 1):
            back = wide_pool[member * 32 : (member + 1) * 32].reshape(1, 2, 1, 16, CH)
            back = jnp.broadcast_to(back, (2, 2, 2, 16, CH)).reshape(128, CH)
            fine = cot_all[member].astype(F32) + back
            grads.append((fine * slope_all[member].astype(F32)).astype(BF16))
        grads = jnp.concatenate(grads, axis=0)
        total = total + jnp.dot(lf[pair].reshape(2 * PART * 32, 256), grads, preferred_element_type=F32)
    both[...] = total.reshape(2, PART * 32, CH)
    send(both.at[1 - core], swapped, 9, mates[1], b)

    row = iota((32, CH), 0)
    own_class = jnp.where(iota((32, CH), 1) == 4 * row + share, 1.0, 0.0).astype(BF16)
    for step in range(PART):
        offset = offset_of(step)
        step_x, step_y, step_z = offset // 9, (offset // 3) % 3, offset % 3
        window = shifted_all[step_z, pl.ds(step_x, GROUPS), step_y + 1].reshape(GROUPS * 16, CH)
        lc[step] = matmul_nt(own_class, window).astype(BF16)
    grads = g_pairs[1 : GROUPS + 1, 1].reshape(GROUPS * 16, CH)
    acc_c[0 : PART * 32] = jnp.dot(lc[...].reshape(PART * 32, 256), grads, preferred_element_type=F32)
    arrived(9)
    acc_f[0 : PART * 32] = both[core] + swapped[...]
    acc_c[PART * 32 :] = jnp.zeros((32, CH), F32)
    acc_f[PART * 32 :] = jnp.zeros((32, CH), F32)

    heard(1)

    def chunk(brick):
        pair = [acc[pl.ds(brick, 8, stride=32), :] for acc in (acc_f, acc_c)]
        rows[brick] = jnp.concatenate(pair, axis=0).astype(BF16)

    for high, step, brick in brick_targets(b):
        chunk(brick)
        send(rows.at[brick], sums.at[high * 16 + step], 7, g, brick)
    chunk(b)
    sums[0] = rows[b]
    output[...] = (act_fine + spread(act_all[g, 8:24], pool)).reshape(2, 4, 16, CH)
    arrived(7)
    fin[g] = jnp.sum(sums[...].astype(F32), axis=0)
    for m in FAR_FIRST:
        send(fin.at[g], fin.at[g], 8, mates[m], b)

    for phase in (0, 1, 2, 3, 4, 5, 6, 7, 9, 10):
        sent(phase)

    arrived(8)
    for member in range(GROUPS):
        channel, part = member // 4, member % 4
        count = PART if part < 3 else PART - 1
        where = pl.ds(part * PART, count)
        grad_fine[where, channel, :] = fin[member, 0:count]
        grad_coarse[where, channel, :] = fin[member, 8 : 8 + count]
    sent(8)


def copy_out(output, grad_fine, grad_coarse, output_to, grad_fine_to, grad_coarse_to, sem):
    copies = [
        pltpu.make_async_copy(src, dst, sem.at[i])
        for i, (src, dst) in enumerate(
            ((output, output_to), (grad_fine, grad_fine_to), (grad_coarse, grad_coarse_to))
        )
    ]
    for copy in copies:
        copy.start()
    for copy in copies:
        copy.wait()


def body(field, cotangent, w_fine, w_coarse):
    anywhere = pl.BlockSpec(memory_space=pl.ANY)
    vmem = pl.BlockSpec(memory_space=pltpu.VMEM)
    fine = (2, 4, 16, CH)
    shapes = (
        jax.ShapeDtypeStruct(fine, F32),
        jax.ShapeDtypeStruct((27, 4, CH), F32),
        jax.ShapeDtypeStruct((27, 4, CH), F32),
    )
    results = pl.pallas_call(
        kernel,
        out_shape=tuple(pltpu.VMEM(shape.shape, shape.dtype) for shape in shapes),
        in_specs=[anywhere] * 4,
        out_specs=(vmem, vmem, vmem),
        scratch_shapes=[
            pltpu.VMEM(fine, F32),
            pltpu.VMEM(fine, F32),
            pltpu.VMEM((9, 3 * CH, CH), BF16),
            pltpu.VMEM((9, 3 * CH, CH), BF16),
            pltpu.VMEM((4, 6, 16, CH), BF16),
            pltpu.VMEM((4, 6, 16, 3 * CH), BF16),
            pltpu.VMEM((32, CH), F32),
            pltpu.VMEM((8 * 32, CH), F32),
            pltpu.VMEM(((GROUPS + 2) * 3, 16, CH), BF16),
            pltpu.VMEM((3, GROUPS + 2, 5, 16, CH), BF16),
            pltpu.VMEM((GROUPS, 32, CH), F32),
            pltpu.VMEM((8, 2, 4, 8, CH), F32),
            pltpu.VMEM((GROUPS + 2, 3, 16, CH), BF16),
            pltpu.VMEM((4, 32, 128), BF16),
            pltpu.VMEM((8, 32, 128), BF16),
            pltpu.VMEM((4, 32, 256), BF16),
            pltpu.VMEM((8, 32, 256), BF16),
            pltpu.VMEM((PART, 384, 256), BF16),
            pltpu.VMEM((8, 128, CH), BF16),
            pltpu.VMEM((8, 128, CH), BF16),
            pltpu.VMEM((4, 2 * PART, 32, 256), BF16),
            pltpu.VMEM((PART, 32, 256), BF16),
            pltpu.VMEM((2, PART * 32, CH), F32),
            pltpu.VMEM((PART * 32, CH), F32),
            pltpu.VMEM((256, CH), F32),
            pltpu.VMEM((256, CH), F32),
            pltpu.VMEM((BRICKS, 16, CH), BF16),
            pltpu.VMEM((BRICKS, 16, CH), BF16),
            pltpu.VMEM((GROUPS, 16, CH), F32),
            pltpu.SemaphoreType.DMA((4,)),
            pltpu.SemaphoreType.DMA((11,)),
            pltpu.SemaphoreType.DMA((11,)),
            pltpu.SemaphoreType.REGULAR((2,)),
        ],
        compiler_params=pltpu.CompilerParams(
            collective_id=0, has_side_effects=True, vmem_limit_bytes=60 * 1024 * 1024
        ),
        cost_estimate=pl.CostEstimate(flops=600_000_000, bytes_accessed=2_500_000, transcendentals=40_000),
        name="unet_levels",
    )(field, cotangent, w_fine.reshape(9, 3 * CH, CH), w_coarse.reshape(9, 3 * CH, CH))
    return pl.pallas_call(
        copy_out,
        out_shape=shapes,
        in_specs=[vmem] * 3,
        out_specs=(anywhere,) * 3,
        scratch_shapes=[pltpu.SemaphoreType.DMA((3,))],
        compiler_params=pltpu.CompilerParams(vmem_limit_bytes=1024 * 1024),
        name="copy_out",
    )(*results)


def solution(mesh):
    in_specs = (P("group", "brick", None, None), P("group", "brick", None, None), P(), P())
    out_specs = (P("group", "brick", None, None), P(None, "brick", None), P(None, "brick", None))
    return jax.shard_map(body, mesh=mesh, in_specs=in_specs, out_specs=out_specs, check_vma=False)
```

```python
import jax
import jax.numpy as jnp
from jax import lax
from jax.experimental import pallas as pl
from jax.experimental.pallas import tpu as pltpu
from jax.sharding import PartitionSpec as P

CH = 128
GROUPS = 16
BRICKS = 32
F32 = jnp.float32
BF16 = jnp.bfloat16
PART = 7
FAR_FIRST = (10, 11, 6, 7, 14, 15, 8, 9, 2, 3, 12, 13, 4, 5, 1)


def brick_targets(b):
    half, ring = b // 16, b % 16
    steps = sorted(range(16), key=lambda step: -min(step, 16 - step))
    return [
        (flip, step, ((half + flip) % 2) * 16 + (ring + step) % 16)
        for step in steps
        for flip in (1, 0)
        if flip or step
    ]


def wait_for(ref, sem):
    pltpu.make_async_copy(ref, ref, sem).wait()


def iota(shape, dim):
    return lax.broadcasted_iota(jnp.int32, shape, dim)


def neighbours_along_depth(rows, depth):
    count = rows.shape[0]
    place = iota(rows.shape, 0) & (depth - 1)
    before = jnp.where(place == 0, 0.0, pltpu.roll(rows, 1, 0))
    after = jnp.where(place == depth - 1, 0.0, pltpu.roll(rows, count - 1, 0))
    return before, after


def matmul_nt(a, b):
    return lax.dot_general(a, b, (((1,), (1,)), ((), ())), preferred_element_type=F32)


def pooled(values, pool):
    pool[...] = jnp.sum(values.reshape(2, 2, 2, 16, CH), axis=(0, 2)).reshape(32, CH)
    return pool[pl.ds(0, 16, stride=2), :] + pool[pl.ds(1, 16, stride=2), :]


def spread(values, pool):
    pool[pl.ds(0, 16, stride=2), :] = values
    pool[pl.ds(1, 16, stride=2), :] = values
    wide = jnp.broadcast_to(pool[...].reshape(1, 2, 1, 16, CH), (2, 2, 2, 16, CH))
    return wide.reshape(128, CH)


def selection(offset):
    row = iota((384, 128), 0)
    cell = iota((384, 128), 1)
    z = cell % 16 + offset % 3 - 1
    y = (cell // 16) % 4 + (offset // 3) % 3
    x = cell // 64 + offset // 9
    own = ((x - 1) * 4 + y - 1) * 16
    side = 320 + (x - 1) * 32 + jnp.where(y == 5, 16, 0)
    source = jnp.where((y == 0) | (y == 5), side, own)
    source = jnp.where(x == 0, 128 + y * 16, jnp.where(x == 3, 224 + y * 16, source))
    hit = (z >= 0) & (z < 16) & (row == source + z)
    return jnp.where(hit, 1.0, 0.0).astype(BF16)


def kernel(
    field, cot, w_fine, w_coarse, output, grad_fine, grad_coarse,
    field_v, cot_v, wf_v, wc_v, ext, ext3, pool, wide_pool, coarse_all, shifted_all, act_all, d_all, g_pairs,
    own_send, own_all, rim_send, rim_all, chosen, cot_all, slope_all, lf, lc, both, swapped, acc_f, acc_c,
    rows, sums, fin,
    local_sem, send_sem, recv_sem, ring_sem,
):
    g = lax.axis_index("group")
    b = lax.axis_index("brick")
    g_up, g_down = (g + 1) % GROUPS, (g + GROUPS - 1) % GROUPS
    b_up, b_down = (b + 1) % BRICKS, (b + BRICKS - 1) % BRICKS
    share, quarter = g // 4, g % 4
    mates = [g + m - 2 * sum(((g // bit) % 2) * bit for bit in (1, 2, 4, 8) if m & bit) for m in range(GROUPS)]

    loads = [
        pltpu.make_async_copy(src, dst, local_sem.at[i])
        for i, (src, dst) in enumerate(((field, field_v), (cot, cot_v), (w_fine, wf_v), (w_coarse, wc_v)))
    ]
    for load in loads:
        load.start()

    barrier = pltpu.get_barrier_semaphore()

    def greet(group, brick):
        pl.semaphore_signal(barrier, inc=1, device_id=(group, brick), device_id_type=pl.DeviceIdType.MESH)

    for m in FAR_FIRST:
        for brick in (b_up, b_down, b):
            greet(mates[m], brick)
    for step in (4, 3, 2, 1):
        greet(g, (b + step) % BRICKS)
        greet(g, (b + BRICKS - step) % BRICKS)

    def tell(stage):
        for step in (4 * 2**stage, BRICKS - 4 * 2**stage):
            pl.semaphore_signal(
                ring_sem.at[stage], inc=1, device_id=(g, (b + step) % BRICKS), device_id_type=pl.DeviceIdType.MESH
            )

    def heard(stage):
        pl.semaphore_wait(ring_sem.at[stage], 2)

    def copy_to(src, dst, send, recv, group, brick):
        return pltpu.make_async_remote_copy(
            src_ref=src,
            dst_ref=dst,
            send_sem=send,
            recv_sem=recv,
            device_id=(group, brick),
            device_id_type=pl.DeviceIdType.MESH,
        )

    def send(src, dst, phase, group, brick):
        copy_to(src, dst, send_sem.at[phase], recv_sem.at[phase], group, brick).start()

    arrivals = (
        ext.at[pl.ds(0, 4), pl.ds(0, 4)],
        cot_all.at[pl.ds(0, 7)],
        wide_pool.at[pl.ds(0, 30 * 8)],
        slope_all.at[pl.ds(0, 7)],
        coarse_all.at[pl.ds(0, 3 * GROUPS - 1)],
        d_all.at[pl.ds(0, 8), 0],
        rim_all.at[pl.ds(0, 7)],
        sums.at[pl.ds(0, BRICKS - 1)],
        fin.at[pl.ds(0, GROUPS - 1)],
        swapped.at[pl.ds(0, PART * 32)],
        own_all.at[pl.ds(0, 7)],
    )

    def arrived(phase):
        wait_for(arrivals[phase], recv_sem.at[phase])

    def sent(phase):
        wait_for(arrivals[phase], send_sem.at[phase])

    chip, core = g // 2, g % 2

    def spread_out(src_of, buf, phase):
        for m in FAR_FIRST:
            if m % 2 == 0:
                send(src_of(mates[m]), buf.at[chip], phase, mates[m], b)

    loads[0].wait()
    ext[1:3, 1:5] = field_v[...].astype(BF16)
    pl.semaphore_wait(barrier, 3 * (GROUPS - 1) + 8)

    send(ext.at[1, 1], ext.at[3, 5], 0, g_down, b_down)
    send(ext.at[1, 4], ext.at[3, 0], 0, g_down, b_up)
    send(ext.at[2, 1], ext.at[0, 5], 0, g_up, b_down)
    send(ext.at[2, 4], ext.at[0, 0], 0, g_up, b_up)
    send(ext.at[1, pl.ds(1, 4)], ext.at[3, pl.ds(1, 4)], 0, g_down, b)
    send(ext.at[2, pl.ds(1, 4)], ext.at[0, pl.ds(1, 4)], 0, g_up, b)
    send(ext.at[pl.ds(1, 2), 1], ext.at[pl.ds(1, 2), 5], 0, g, b_down)
    send(ext.at[pl.ds(1, 2), 4], ext.at[pl.ds(1, 2), 0], 0, g, b_up)

    tell(0)

    loads[1].wait()
    cot_rows = cot_v[...].reshape(128, CH)
    cot_all[chip] = cot_rows.astype(BF16)
    spread_out(lambda mate: cot_all.at[chip], cot_all, 1)
    d_all[chip, core, 1:3] = pooled(cot_rows, pool).reshape(2, 8, CH)
    for m in FAR_FIRST + (0,):
        if m % 2 == 0:
            send(d_all.at[chip, core, 1], d_all.at[chip, core, 3], 2, mates[m], b_down)
            send(d_all.at[chip, core, 2], d_all.at[chip, core, 0], 2, mates[m], b_up)
            if m:
                send(d_all.at[chip, core, pl.ds(1, 2)], d_all.at[chip, core, pl.ds(1, 2)], 2, mates[m], b)
    for row in (0, 1, 2, 51, 52, 53):
        coarse_all[row] = jnp.zeros((16, CH), BF16)
    order = iota((CH, CH), 0)
    sort = jnp.where(iota((CH, CH), 1) == 4 * (order % 32) + order // 32, 1.0, 0.0).astype(BF16)
    own_send[...] = matmul_nt(sort, ext[1:3, 1:5].reshape(128, CH)).astype(BF16).reshape(4, 32, 128)
    spread_out(lambda mate: own_send.at[mate // 4], own_all, 10)
    own_all[chip] = own_send[share]

    def offset_of(step):
        return quarter * PART + step - (quarter // 3 if step == PART - 1 else 0)

    half = quarter // 2
    for step in range(0, 2 * PART, 2):
        offset = half * 2 * PART + step
        later = offset + 1 - (half if step + 1 == 2 * PART - 1 else 0)
        chosen[step // 2, :, 0:128] = selection(offset)
        chosen[step // 2, :, 128:256] = selection(later)
    loads[2].wait()
    loads[3].wait()

    arrived(0)

    def clear(outside, part):
        @pl.when(outside)
        def _():
            ext[part] = jnp.zeros(ext.at[part].shape, BF16)

    clear(g == 0, slice(0, 1))
    clear(g == GROUPS - 1, slice(3, 4))
    clear(b == 0, (slice(0, 4), slice(0, 1)))
    clear(b == BRICKS - 1, (slice(0, 4), slice(5, 6)))

    cells = ext[...].reshape(384, CH)
    rim = [ext[0].reshape(96, CH), ext[3].reshape(96, CH), ext[1, 0], ext[1, 5], ext[2, 0], ext[2, 5]]
    rim_send[...] = matmul_nt(sort, jnp.concatenate(rim, axis=0)).astype(BF16).reshape(4, 32, 256)
    spread_out(lambda mate: rim_send.at[mate // 4], rim_all, 6)
    rim_all[chip] = rim_send[share]

    before, after = neighbours_along_depth(cells.astype(F32), 16)
    ext3[:, :, :, 0:CH] = before.astype(BF16).reshape(4, 6, 16, CH)
    ext3[:, :, :, CH : 2 * CH] = ext[...]
    ext3[:, :, :, 2 * CH :] = after.astype(BF16).reshape(4, 6, 16, CH)

    z_fine = jnp.zeros((128, CH), F32)
    for step in range(9):
        step_x, step_y = step // 3, step % 3
        window = ext3[step_x : step_x + 2, step_y : step_y + 4].reshape(128, 3 * CH)
        z_fine = z_fine + jnp.dot(window, wf_v[step], preferred_element_type=F32)
    sig = jax.nn.sigmoid(z_fine)
    act_fine = z_fine * sig
    slope_fine = sig * (1.0 + z_fine * (1.0 - sig))
    coarse = (pooled(act_fine, pool) * 0.125).astype(BF16)

    own = (g + 1) * 3
    coarse_all[own + 1] = coarse
    for m in FAR_FIRST + (0,):
        send(coarse_all.at[own + 1], coarse_all.at[own + 2], 4, mates[m], b_down)
        send(coarse_all.at[own + 1], coarse_all.at[own], 4, mates[m], b_up)
        if m:
            send(coarse_all.at[own + 1], coarse_all.at[own + 1], 4, mates[m], b)

    slope_all[chip] = slope_fine.astype(BF16)
    spread_out(lambda mate: slope_all.at[chip], slope_all, 3)

    heard(0)
    tell(1)
    arrived(2)
    send(d_all.at[:, core], d_all.at[:, core], 5, mates[1], b)

    arrived(10)
    arrived(6)
    everyone = jnp.concatenate([own_all[...], rim_all[...]], axis=2).reshape(8 * 32, 384)
    for step in range(0, 2 * PART, 2):
        picked = jnp.dot(everyone, chosen[step // 2], preferred_element_type=F32).astype(BF16).reshape(4, 2, 32, 256)
        for i in range(2):
            for member in range(2):
                lf[:, step + i, :, member * 128 : (member + 1) * 128] = picked[:, member, :, i * 128 : (i + 1) * 128]
    arrived(1)
    arrived(5)
    arrived(4)

    def clear_sides(outside, place):
        @pl.when(outside)
        def _():
            for x in range(GROUPS):
                coarse_all[(x + 1) * 3 + place] = jnp.zeros((16, CH), BF16)

    clear_sides(b == 0, 0)
    clear_sides(b == BRICKS - 1, 2)

    ccells = coarse_all[...].astype(F32).reshape((GROUPS + 2) * 48, CH)
    before, after = neighbours_along_depth(ccells, 8)
    for step_z, shifted in enumerate((before, ccells, after)):
        shifted = shifted.reshape(GROUPS + 2, 6, 8, CH)
        for y in range(5):
            shifted_all[step_z, :, y] = shifted[:, y : y + 2].reshape(GROUPS + 2, 16, CH).astype(BF16)
    z_coarse = jnp.zeros((GROUPS * 32, CH), F32)
    for step in range(9):
        step_x, step_y = step // 3, step % 3
        window = [
            jnp.concatenate(
                [shifted_all[step_z, step_x : step_x + GROUPS, step_y + y][:, None] for y in (0, 2)], axis=1
            ).reshape(GROUPS * 32, CH)
            for step_z in range(3)
        ]
        window = jnp.concatenate(window, axis=1)
        z_coarse = z_coarse + jnp.dot(window, wc_v[step], preferred_element_type=F32)
    sig = jax.nn.sigmoid(z_coarse)
    act_all[...] = (z_coarse * sig).reshape(GROUPS, 32, CH)
    d_coarse = d_all[...].reshape(GROUPS * 32, CH)
    row = iota((GROUPS * 32, CH), 0) % 32
    outside = ((row < 8) & (b == 0)) | ((row >= 24) & (b == BRICKS - 1))
    d_coarse = jnp.where(outside, 0.0, d_coarse)
    g_coarse = d_coarse * (sig * (1.0 + z_coarse * (1.0 - sig)))
    g_coarse = g_coarse.astype(BF16).astype(F32).reshape(GROUPS, 4, 8, CH)
    g_pairs[0] = jnp.zeros((3, 16, CH), BF16)
    g_pairs[GROUPS + 1] = jnp.zeros((3, 16, CH), BF16)
    for y in range(3):
        g_pairs[1 : GROUPS + 1, y] = g_coarse[:, y : y + 2].reshape(GROUPS, 16, CH).astype(BF16)

    mixed = jnp.zeros((8 * 16, 3 * CH), F32)
    for step in range(9):
        step_x, step_y = step // 3, step % 3
        window = jnp.concatenate([g_pairs[2 * member + core + 2 - step_x, 2 - step_y] for member in range(8)], axis=0)
        mixed = mixed + matmul_nt(window, wc_v[step])
    back_coarse = mixed[:, CH : 2 * CH]
    back_coarse = back_coarse + neighbours_along_depth(mixed[:, 0:CH], 8)[1]
    back_coarse = back_coarse + neighbours_along_depth(mixed[:, 2 * CH :], 8)[0]
    back_coarse = back_coarse * 0.125
    wide_pool[pl.ds(0, 8 * 16, stride=2), :] = back_coarse
    wide_pool[pl.ds(1, 8 * 16, stride=2), :] = back_coarse
    arrived(3)
    total = jnp.zeros((2 * PART * 32, CH), F32)
    for pair in range(4):
        grads = []
        for member in (2 * pair, 2 * pair + 1):
            back = wide_pool[member * 32 : (member + 1) * 32].reshape(1, 2, 1, 16, CH)
            back = jnp.broadcast_to(back, (2, 2, 2, 16, CH)).reshape(128, CH)
            fine = cot_all[member].astype(F32) + back
            grads.append((fine * slope_all[member].astype(F32)).astype(BF16))
        grads = jnp.concatenate(grads, axis=0)
        total = total + jnp.dot(lf[pair].reshape(2 * PART * 32, 256), grads, preferred_element_type=F32)
    both[...] = total.reshape(2, PART * 32, CH)
    send(both.at[1 - core], swapped, 9, mates[1], b)

    row = iota((32, CH), 0)
    own_class = jnp.where(iota((32, CH), 1) == 4 * row + share, 1.0, 0.0).astype(BF16)
    for step in range(PART):
        offset = offset_of(step)
        step_x, step_y, step_z = offset // 9, (offset // 3) % 3, offset % 3
        window = shifted_all[step_z, pl.ds(step_x, GROUPS), step_y + 1].reshape(GROUPS * 16, CH)
        lc[step] = matmul_nt(own_class, window).astype(BF16)
    grads = g_pairs[1 : GROUPS + 1, 1].reshape(GROUPS * 16, CH)
    acc_c[0 : PART * 32] = jnp.dot(lc[...].reshape(PART * 32, 256), grads, preferred_element_type=F32)
    arrived(9)
    acc_f[0 : PART * 32] = both[core] + swapped[...]
    acc_c[PART * 32 :] = jnp.zeros((32, CH), F32)
    acc_f[PART * 32 :] = jnp.zeros((32, CH), F32)

    heard(1)

    def chunk(brick):
        pair = [acc[pl.ds(brick, 8, stride=32), :] for acc in (acc_f, acc_c)]
        rows[brick] = jnp.concatenate(pair, axis=0).astype(BF16)

    for high, step, brick in brick_targets(b):
        chunk(brick)
        send(rows.at[brick], sums.at[high * 16 + step], 7, g, brick)
    chunk(b)
    sums[0] = rows[b]
    output[...] = (act_fine + spread(act_all[g, 8:24], pool)).reshape(2, 4, 16, CH)
    arrived(7)
    fin[g] = jnp.sum(sums[...].astype(F32), axis=0).astype(BF16)
    for m in FAR_FIRST:
        send(fin.at[g], fin.at[g], 8, mates[m], b)

    for phase in (0, 1, 2, 3, 4, 5, 6, 7, 9, 10):
        sent(phase)

    arrived(8)
    for member in range(GROUPS):
        channel, part = member // 4, member % 4
        count = PART if part < 3 else PART - 1
        where = pl.ds(part * PART, count)
        share_rows = fin[member].astype(F32)
        grad_fine[where, channel, :] = share_rows[0:count]
        grad_coarse[where, channel, :] = share_rows[8 : 8 + count]
    sent(8)


def copy_out(output, grad_fine, grad_coarse, output_to, grad_fine_to, grad_coarse_to, sem):
    copies = [
        pltpu.make_async_copy(src, dst, sem.at[i])
        for i, (src, dst) in enumerate(
            ((output, output_to), (grad_fine, grad_fine_to), (grad_coarse, grad_coarse_to))
        )
    ]
    for copy in copies:
        copy.start()
    for copy in copies:
        copy.wait()


def body(field, cotangent, w_fine, w_coarse):
    anywhere = pl.BlockSpec(memory_space=pl.ANY)
    vmem = pl.BlockSpec(memory_space=pltpu.VMEM)
    fine = (2, 4, 16, CH)
    shapes = (
        jax.ShapeDtypeStruct(fine, F32),
        jax.ShapeDtypeStruct((27, 4, CH), F32),
        jax.ShapeDtypeStruct((27, 4, CH), F32),
    )
    results = pl.pallas_call(
        kernel,
        out_shape=tuple(pltpu.VMEM(shape.shape, shape.dtype) for shape in shapes),
        in_specs=[anywhere] * 4,
        out_specs=(vmem, vmem, vmem),
        scratch_shapes=[
            pltpu.VMEM(fine, F32),
            pltpu.VMEM(fine, F32),
            pltpu.VMEM((9, 3 * CH, CH), BF16),
            pltpu.VMEM((9, 3 * CH, CH), BF16),
            pltpu.VMEM((4, 6, 16, CH), BF16),
            pltpu.VMEM((4, 6, 16, 3 * CH), BF16),
            pltpu.VMEM((32, CH), F32),
            pltpu.VMEM((8 * 32, CH), F32),
            pltpu.VMEM(((GROUPS + 2) * 3, 16, CH), BF16),
            pltpu.VMEM((3, GROUPS + 2, 5, 16, CH), BF16),
            pltpu.VMEM((GROUPS, 32, CH), F32),
            pltpu.VMEM((8, 2, 4, 8, CH), F32),
            pltpu.VMEM((GROUPS + 2, 3, 16, CH), BF16),
            pltpu.VMEM((4, 32, 128), BF16),
            pltpu.VMEM((8, 32, 128), BF16),
            pltpu.VMEM((4, 32, 256), BF16),
            pltpu.VMEM((8, 32, 256), BF16),
            pltpu.VMEM((PART, 384, 256), BF16),
            pltpu.VMEM((8, 128, CH), BF16),
            pltpu.VMEM((8, 128, CH), BF16),
            pltpu.VMEM((4, 2 * PART, 32, 256), BF16),
            pltpu.VMEM((PART, 32, 256), BF16),
            pltpu.VMEM((2, PART * 32, CH), F32),
            pltpu.VMEM((PART * 32, CH), F32),
            pltpu.VMEM((256, CH), F32),
            pltpu.VMEM((256, CH), F32),
            pltpu.VMEM((BRICKS, 16, CH), BF16),
            pltpu.VMEM((BRICKS, 16, CH), BF16),
            pltpu.VMEM((GROUPS, 16, CH), BF16),
            pltpu.SemaphoreType.DMA((4,)),
            pltpu.SemaphoreType.DMA((11,)),
            pltpu.SemaphoreType.DMA((11,)),
            pltpu.SemaphoreType.REGULAR((2,)),
        ],
        compiler_params=pltpu.CompilerParams(
            collective_id=0, has_side_effects=True, vmem_limit_bytes=60 * 1024 * 1024
        ),
        cost_estimate=pl.CostEstimate(flops=600_000_000, bytes_accessed=2_500_000, transcendentals=40_000),
        name="unet_levels",
    )(field, cotangent, w_fine.reshape(9, 3 * CH, CH), w_coarse.reshape(9, 3 * CH, CH))
    return pl.pallas_call(
        copy_out,
        out_shape=shapes,
        in_specs=[vmem] * 3,
        out_specs=(anywhere,) * 3,
        scratch_shapes=[pltpu.SemaphoreType.DMA((3,))],
        compiler_params=pltpu.CompilerParams(vmem_limit_bytes=1024 * 1024),
        name="copy_out",
    )(*results)


def solution(mesh):
    in_specs = (P("group", "brick", None, None), P("group", "brick", None, None), P(), P())
    out_specs = (P("group", "brick", None, None), P(None, "brick", None), P(None, "brick", None))
    return jax.shard_map(body, mesh=mesh, in_specs=in_specs, out_specs=out_specs, check_vma=False)
```

```python
import jax
import jax.numpy as jnp
from jax import lax
from jax.experimental import pallas as pl
from jax.experimental.pallas import tpu as pltpu
from jax.sharding import PartitionSpec as P

CH = 128
GROUPS = 16
BRICKS = 32
F32 = jnp.float32
BF16 = jnp.bfloat16
PART = 7
FAR_FIRST = (10, 11, 6, 7, 14, 15, 8, 9, 2, 3, 12, 13, 4, 5, 1)


def brick_targets(b):
    half, ring = b // 16, b % 16
    steps = sorted(range(16), key=lambda step: -min(step, 16 - step))
    return [
        (flip, step, ((half + flip) % 2) * 16 + (ring + step) % 16)
        for step in steps
        for flip in (1, 0)
        if flip or step
    ]


def wait_for(ref, sem):
    pltpu.make_async_copy(ref, ref, sem).wait()


def iota(shape, dim):
    return lax.broadcasted_iota(jnp.int32, shape, dim)


def neighbours_along_depth(rows, depth):
    count = rows.shape[0]
    place = iota(rows.shape, 0) & (depth - 1)
    before = jnp.where(place == 0, 0.0, pltpu.roll(rows, 1, 0))
    after = jnp.where(place == depth - 1, 0.0, pltpu.roll(rows, count - 1, 0))
    return before, after


def matmul_nt(a, b):
    return lax.dot_general(a, b, (((1,), (1,)), ((), ())), preferred_element_type=F32)


def pooled(values, pool):
    pool[...] = jnp.sum(values.reshape(2, 2, 2, 16, CH), axis=(0, 2)).reshape(32, CH)
    return pool[pl.ds(0, 16, stride=2), :] + pool[pl.ds(1, 16, stride=2), :]


def spread(values, pool):
    pool[pl.ds(0, 16, stride=2), :] = values
    pool[pl.ds(1, 16, stride=2), :] = values
    wide = jnp.broadcast_to(pool[...].reshape(1, 2, 1, 16, CH), (2, 2, 2, 16, CH))
    return wide.reshape(128, CH)


def selection(offset):
    row = iota((384, 128), 0)
    cell = iota((384, 128), 1)
    z = cell % 16 + offset % 3 - 1
    y = (cell // 16) % 4 + (offset // 3) % 3
    x = cell // 64 + offset // 9
    own = ((x - 1) * 4 + y - 1) * 16
    side = 320 + (x - 1) * 32 + jnp.where(y == 5, 16, 0)
    source = jnp.where((y == 0) | (y == 5), side, own)
    source = jnp.where(x == 0, 128 + y * 16, jnp.where(x == 3, 224 + y * 16, source))
    hit = (z >= 0) & (z < 16) & (row == source + z)
    return jnp.where(hit, 1.0, 0.0).astype(BF16)


def kernel(
    field, cot, w_fine, w_coarse, output, grad_fine, grad_coarse,
    field_v, cot_v, wf_v, wc_v, ext, ext3, pool, wide_pool, coarse_all, shifted_all, act_all, d_all, g_pairs,
    own_send, own_all, rim_send, rim_all, chosen, cot_all, slope_all, lf, lc, both, swapped, acc_f, acc_c,
    rows, sums, fin,
    local_sem, send_sem, recv_sem, ring_sem,
):
    g = lax.axis_index("group")
    b = lax.axis_index("brick")
    g_up, g_down = (g + 1) % GROUPS, (g + GROUPS - 1) % GROUPS
    b_up, b_down = (b + 1) % BRICKS, (b + BRICKS - 1) % BRICKS
    share, quarter = g // 4, g % 4
    mates = [g + m - 2 * sum(((g // bit) % 2) * bit for bit in (1, 2, 4, 8) if m & bit) for m in range(GROUPS)]

    loads = [
        pltpu.make_async_copy(src, dst, local_sem.at[i])
        for i, (src, dst) in enumerate(((field, field_v), (cot, cot_v), (w_fine, wf_v), (w_coarse, wc_v)))
    ]
    for load in loads:
        load.start()

    barrier = pltpu.get_barrier_semaphore()

    def greet(group, brick):
        pl.semaphore_signal(barrier, inc=1, device_id=(group, brick), device_id_type=pl.DeviceIdType.MESH)

    for m in FAR_FIRST:
        for brick in (b_up, b_down, b):
            greet(mates[m], brick)
    for step in (4, 3, 2, 1):
        greet(g, (b + step) % BRICKS)
        greet(g, (b + BRICKS - step) % BRICKS)

    def tell(stage):
        for step in (4 * 2**stage, BRICKS - 4 * 2**stage):
            pl.semaphore_signal(
                ring_sem.at[stage], inc=1, device_id=(g, (b + step) % BRICKS), device_id_type=pl.DeviceIdType.MESH
            )

    def heard(stage):
        pl.semaphore_wait(ring_sem.at[stage], 2)

    def copy_to(src, dst, send, recv, group, brick):
        return pltpu.make_async_remote_copy(
            src_ref=src,
            dst_ref=dst,
            send_sem=send,
            recv_sem=recv,
            device_id=(group, brick),
            device_id_type=pl.DeviceIdType.MESH,
        )

    def send(src, dst, phase, group, brick):
        copy_to(src, dst, send_sem.at[phase], recv_sem.at[phase], group, brick).start()

    arrivals = (
        ext.at[pl.ds(0, 4), pl.ds(0, 4)],
        cot_all.at[pl.ds(0, 7)],
        wide_pool.at[pl.ds(0, 30 * 8)],
        slope_all.at[pl.ds(0, 7)],
        coarse_all.at[pl.ds(0, 3 * GROUPS - 1)],
        d_all.at[pl.ds(0, 8), 0],
        rim_all.at[pl.ds(0, 7)],
        sums.at[pl.ds(0, BRICKS - 1)],
        fin.at[pl.ds(0, GROUPS - 1)],
        swapped.at[pl.ds(0, PART * 32)],
        own_all.at[pl.ds(0, 7)],
    )

    def arrived(phase):
        wait_for(arrivals[phase], recv_sem.at[phase])

    def sent(phase):
        wait_for(arrivals[phase], send_sem.at[phase])

    chip, core = g // 2, g % 2

    def spread_out(src_of, buf, phase):
        for m in FAR_FIRST:
            if m % 2 == 0:
                send(src_of(mates[m]), buf.at[chip], phase, mates[m], b)

    loads[0].wait()
    ext[1:3, 1:5] = field_v[...].astype(BF16)
    pl.semaphore_wait(barrier, 3 * (GROUPS - 1) + 8)

    send(ext.at[1, 1], ext.at[3, 5], 0, g_down, b_down)
    send(ext.at[1, 4], ext.at[3, 0], 0, g_down, b_up)
    send(ext.at[2, 1], ext.at[0, 5], 0, g_up, b_down)
    send(ext.at[2, 4], ext.at[0, 0], 0, g_up, b_up)
    send(ext.at[1, pl.ds(1, 4)], ext.at[3, pl.ds(1, 4)], 0, g_down, b)
    send(ext.at[2, pl.ds(1, 4)], ext.at[0, pl.ds(1, 4)], 0, g_up, b)
    send(ext.at[pl.ds(1, 2), 1], ext.at[pl.ds(1, 2), 5], 0, g, b_down)
    send(ext.at[pl.ds(1, 2), 4], ext.at[pl.ds(1, 2), 0], 0, g, b_up)

    tell(0)

    loads[1].wait()
    cot_rows = cot_v[...].reshape(128, CH)
    cot_all[chip] = cot_rows.astype(BF16)
    spread_out(lambda mate: cot_all.at[chip], cot_all, 1)
    d_all[chip, core, 1:3] = pooled(cot_rows, pool).reshape(2, 8, CH)
    for m in FAR_FIRST + (0,):
        if m % 2 == 0:
            send(d_all.at[chip, core, 1], d_all.at[chip, core, 3], 2, mates[m], b_down)
            send(d_all.at[chip, core, 2], d_all.at[chip, core, 0], 2, mates[m], b_up)
            if m:
                send(d_all.at[chip, core, pl.ds(1, 2)], d_all.at[chip, core, pl.ds(1, 2)], 2, mates[m], b)
    for row in (0, 1, 2, 51, 52, 53):
        coarse_all[row] = jnp.zeros((16, CH), BF16)
    order = iota((CH, CH), 0)
    sort = jnp.where(iota((CH, CH), 1) == 4 * (order % 32) + order // 32, 1.0, 0.0).astype(BF16)
    own_send[...] = matmul_nt(sort, ext[1:3, 1:5].reshape(128, CH)).astype(BF16).reshape(4, 32, 128)
    spread_out(lambda mate: own_send.at[mate // 4], own_all, 10)
    own_all[chip] = own_send[share]

    def offset_of(step):
        return quarter * PART + step - (quarter // 3 if step == PART - 1 else 0)

    half = quarter // 2
    for step in range(0, 2 * PART, 2):
        offset = half * 2 * PART + step
        later = offset + 1 - (half if step + 1 == 2 * PART - 1 else 0)
        chosen[step // 2, :, 0:128] = selection(offset)
        chosen[step // 2, :, 128:256] = selection(later)
    loads[2].wait()
    loads[3].wait()

    arrived(0)

    def clear(outside, part):
        @pl.when(outside)
        def _():
            ext[part] = jnp.zeros(ext.at[part].shape, BF16)

    clear(g == 0, slice(0, 1))
    clear(g == GROUPS - 1, slice(3, 4))
    clear(b == 0, (slice(0, 4), slice(0, 1)))
    clear(b == BRICKS - 1, (slice(0, 4), slice(5, 6)))

    cells = ext[...].reshape(384, CH)
    rim = [ext[0].reshape(96, CH), ext[3].reshape(96, CH), ext[1, 0], ext[1, 5], ext[2, 0], ext[2, 5]]
    rim_send[...] = matmul_nt(sort, jnp.concatenate(rim, axis=0)).astype(BF16).reshape(4, 32, 256)
    spread_out(lambda mate: rim_send.at[mate // 4], rim_all, 6)
    rim_all[chip] = rim_send[share]

    before, after = neighbours_along_depth(cells.astype(F32), 16)
    ext3[:, :, :, 0:CH] = before.astype(BF16).reshape(4, 6, 16, CH)
    ext3[:, :, :, CH : 2 * CH] = ext[...]
    ext3[:, :, :, 2 * CH :] = after.astype(BF16).reshape(4, 6, 16, CH)

    z_fine = jnp.zeros((128, CH), F32)
    for step in range(9):
        step_x, step_y = step // 3, step % 3
        window = ext3[step_x : step_x + 2, step_y : step_y + 4].reshape(128, 3 * CH)
        z_fine = z_fine + jnp.dot(window, wf_v[step], preferred_element_type=F32)
    sig = jax.nn.sigmoid(z_fine)
    act_fine = z_fine * sig
    slope_fine = sig * (1.0 + z_fine * (1.0 - sig))
    coarse = (pooled(act_fine, pool) * 0.125).astype(BF16)

    own = (g + 1) * 3
    coarse_all[own + 1] = coarse
    for m in FAR_FIRST + (0,):
        send(coarse_all.at[own + 1], coarse_all.at[own + 2], 4, mates[m], b_down)
        send(coarse_all.at[own + 1], coarse_all.at[own], 4, mates[m], b_up)
        if m:
            send(coarse_all.at[own + 1], coarse_all.at[own + 1], 4, mates[m], b)

    slope_all[chip] = slope_fine.astype(BF16)
    spread_out(lambda mate: slope_all.at[chip], slope_all, 3)

    heard(0)
    tell(1)
    arrived(2)
    send(d_all.at[:, core], d_all.at[:, core], 5, mates[1], b)

    arrived(10)
    arrived(6)
    everyone = jnp.concatenate([own_all[...], rim_all[...]], axis=2).reshape(8 * 32, 384)
    for step in range(0, 2 * PART, 2):
        picked = jnp.dot(everyone, chosen[step // 2], preferred_element_type=F32).astype(BF16).reshape(4, 2, 32, 256)
        for i in range(2):
            for member in range(2):
                lf[:, step + i, :, member * 128 : (member + 1) * 128] = picked[:, member, :, i * 128 : (i + 1) * 128]
    arrived(1)
    arrived(5)
    arrived(4)

    def clear_sides(outside, place):
        @pl.when(outside)
        def _():
            for x in range(GROUPS):
                coarse_all[(x + 1) * 3 + place] = jnp.zeros((16, CH), BF16)

    clear_sides(b == 0, 0)
    clear_sides(b == BRICKS - 1, 2)

    ccells = coarse_all[...].astype(F32).reshape((GROUPS + 2) * 48, CH)
    before, after = neighbours_along_depth(ccells, 8)
    for step_z, shifted in enumerate((before, ccells, after)):
        shifted = shifted.reshape(GROUPS + 2, 6, 8, CH)
        for y in range(5):
            shifted_all[step_z, :, y] = shifted[:, y : y + 2].reshape(GROUPS + 2, 16, CH).astype(BF16)
    z_coarse = jnp.zeros((GROUPS * 32, CH), F32)
    for step in range(9):
        step_x, step_y = step // 3, step % 3
        window = [
            jnp.concatenate(
                [shifted_all[step_z, step_x : step_x + GROUPS, step_y + y][:, None] for y in (0, 2)], axis=1
            ).reshape(GROUPS * 32, CH)
            for step_z in range(3)
        ]
        window = jnp.concatenate(window, axis=1)
        z_coarse = z_coarse + jnp.dot(window, wc_v[step], preferred_element_type=F32)
    sig = jax.nn.sigmoid(z_coarse)
    act_all[...] = (z_coarse * sig).reshape(GROUPS, 32, CH)
    d_coarse = d_all[...].reshape(GROUPS * 32, CH)
    row = iota((GROUPS * 32, CH), 0) % 32
    outside = ((row < 8) & (b == 0)) | ((row >= 24) & (b == BRICKS - 1))
    d_coarse = jnp.where(outside, 0.0, d_coarse)
    g_coarse = d_coarse * (sig * (1.0 + z_coarse * (1.0 - sig)))
    g_coarse = g_coarse.astype(BF16).astype(F32).reshape(GROUPS, 4, 8, CH)
    g_pairs[0] = jnp.zeros((3, 16, CH), BF16)
    g_pairs[GROUPS + 1] = jnp.zeros((3, 16, CH), BF16)
    for y in range(3):
        g_pairs[1 : GROUPS + 1, y] = g_coarse[:, y : y + 2].reshape(GROUPS, 16, CH).astype(BF16)

    mixed = jnp.zeros((8 * 16, 3 * CH), F32)
    for step in range(9):
        step_x, step_y = step // 3, step % 3
        window = jnp.concatenate([g_pairs[2 * member + core + 2 - step_x, 2 - step_y] for member in range(8)], axis=0)
        mixed = mixed + matmul_nt(window, wc_v[step])
    back_coarse = mixed[:, CH : 2 * CH]
    back_coarse = back_coarse + neighbours_along_depth(mixed[:, 0:CH], 8)[1]
    back_coarse = back_coarse + neighbours_along_depth(mixed[:, 2 * CH :], 8)[0]
    back_coarse = back_coarse * 0.125
    wide_pool[pl.ds(0, 8 * 16, stride=2), :] = back_coarse
    wide_pool[pl.ds(1, 8 * 16, stride=2), :] = back_coarse
    arrived(3)
    total = jnp.zeros((2 * PART * 32, CH), F32)
    for pair in range(4):
        grads = []
        for member in (2 * pair, 2 * pair + 1):
            back = wide_pool[member * 32 : (member + 1) * 32].reshape(1, 2, 1, 16, CH)
            back = jnp.broadcast_to(back, (2, 2, 2, 16, CH)).reshape(128, CH)
            fine = cot_all[member].astype(F32) + back
            grads.append((fine * slope_all[member].astype(F32)).astype(BF16))
        grads = jnp.concatenate(grads, axis=0)
        total = total + jnp.dot(lf[pair].reshape(2 * PART * 32, 256), grads, preferred_element_type=F32)
    both[...] = total.reshape(2, PART * 32, CH)
    send(both.at[1 - core], swapped, 9, mates[1], b)

    row = iota((32, CH), 0)
    own_class = jnp.where(iota((32, CH), 1) == 4 * row + share, 1.0, 0.0).astype(BF16)
    for step in range(PART):
        offset = offset_of(step)
        step_x, step_y, step_z = offset // 9, (offset // 3) % 3, offset % 3
        window = shifted_all[step_z, pl.ds(step_x, GROUPS), step_y + 1].reshape(GROUPS * 16, CH)
        lc[step] = matmul_nt(own_class, window).astype(BF16)
    grads = g_pairs[1 : GROUPS + 1, 1].reshape(GROUPS * 16, CH)
    acc_c[0 : PART * 32] = jnp.dot(lc[...].reshape(PART * 32, 256), grads, preferred_element_type=F32)
    arrived(9)
    acc_f[0 : PART * 32] = both[core] + swapped[...]
    acc_c[PART * 32 :] = jnp.zeros((32, CH), F32)
    acc_f[PART * 32 :] = jnp.zeros((32, CH), F32)

    heard(1)

    def chunk(brick):
        pair = [acc[pl.ds(brick, 8, stride=32), :] for acc in (acc_f, acc_c)]
        rows[brick] = jnp.concatenate(pair, axis=0).astype(BF16)

    for high, step, brick in brick_targets(b):
        chunk(brick)
        send(rows.at[brick], sums.at[high * 16 + step], 7, g, brick)
    chunk(b)
    sums[0] = rows[b]
    output[...] = (act_fine + spread(act_all[g, 8:24], pool)).reshape(2, 4, 16, CH)
    arrived(7)
    fin[g] = jnp.sum(sums[...].astype(F32), axis=0)
    for m in FAR_FIRST:
        send(fin.at[g], fin.at[g], 8, mates[m], b)

    for phase in (0, 1, 2, 3, 4, 5, 6, 7, 9, 10):
        sent(phase)

    arrived(8)
    for part in range(4):
        count = PART if part < 3 else PART - 1
        where = pl.ds(part * PART, count)
        shares = [fin[channel * 4 + part] for channel in range(4)]
        grad_fine[where] = jnp.stack([share[0:count] for share in shares], axis=1)
        grad_coarse[where] = jnp.stack([share[8 : 8 + count] for share in shares], axis=1)
    sent(8)


def copy_out(output, grad_fine, grad_coarse, output_to, grad_fine_to, grad_coarse_to, sem):
    copies = [
        pltpu.make_async_copy(src, dst, sem.at[i])
        for i, (src, dst) in enumerate(
            ((output, output_to), (grad_fine, grad_fine_to), (grad_coarse, grad_coarse_to))
        )
    ]
    for copy in copies:
        copy.start()
    for copy in copies:
        copy.wait()


def body(field, cotangent, w_fine, w_coarse):
    anywhere = pl.BlockSpec(memory_space=pl.ANY)
    vmem = pl.BlockSpec(memory_space=pltpu.VMEM)
    fine = (2, 4, 16, CH)
    shapes = (
        jax.ShapeDtypeStruct(fine, F32),
        jax.ShapeDtypeStruct((27, 4, CH), F32),
        jax.ShapeDtypeStruct((27, 4, CH), F32),
    )
    results = pl.pallas_call(
        kernel,
        out_shape=tuple(pltpu.VMEM(shape.shape, shape.dtype) for shape in shapes),
        in_specs=[anywhere] * 4,
        out_specs=(vmem, vmem, vmem),
        scratch_shapes=[
            pltpu.VMEM(fine, F32),
            pltpu.VMEM(fine, F32),
            pltpu.VMEM((9, 3 * CH, CH), BF16),
            pltpu.VMEM((9, 3 * CH, CH), BF16),
            pltpu.VMEM((4, 6, 16, CH), BF16),
            pltpu.VMEM((4, 6, 16, 3 * CH), BF16),
            pltpu.VMEM((32, CH), F32),
            pltpu.VMEM((8 * 32, CH), F32),
            pltpu.VMEM(((GROUPS + 2) * 3, 16, CH), BF16),
            pltpu.VMEM((3, GROUPS + 2, 5, 16, CH), BF16),
            pltpu.VMEM((GROUPS, 32, CH), F32),
            pltpu.VMEM((8, 2, 4, 8, CH), F32),
            pltpu.VMEM((GROUPS + 2, 3, 16, CH), BF16),
            pltpu.VMEM((4, 32, 128), BF16),
            pltpu.VMEM((8, 32, 128), BF16),
            pltpu.VMEM((4, 32, 256), BF16),
            pltpu.VMEM((8, 32, 256), BF16),
            pltpu.VMEM((PART, 384, 256), BF16),
            pltpu.VMEM((8, 128, CH), BF16),
            pltpu.VMEM((8, 128, CH), BF16),
            pltpu.VMEM((4, 2 * PART, 32, 256), BF16),
            pltpu.VMEM((PART, 32, 256), BF16),
            pltpu.VMEM((2, PART * 32, CH), F32),
            pltpu.VMEM((PART * 32, CH), F32),
            pltpu.VMEM((256, CH), F32),
            pltpu.VMEM((256, CH), F32),
            pltpu.VMEM((BRICKS, 16, CH), BF16),
            pltpu.VMEM((BRICKS, 16, CH), BF16),
            pltpu.VMEM((GROUPS, 16, CH), F32),
            pltpu.SemaphoreType.DMA((4,)),
            pltpu.SemaphoreType.DMA((11,)),
            pltpu.SemaphoreType.DMA((11,)),
            pltpu.SemaphoreType.REGULAR((2,)),
        ],
        compiler_params=pltpu.CompilerParams(
            collective_id=0, has_side_effects=True, vmem_limit_bytes=60 * 1024 * 1024
        ),
        cost_estimate=pl.CostEstimate(flops=600_000_000, bytes_accessed=2_500_000, transcendentals=40_000),
        name="unet_levels",
    )(field, cotangent, w_fine.reshape(9, 3 * CH, CH), w_coarse.reshape(9, 3 * CH, CH))
    return pl.pallas_call(
        copy_out,
        out_shape=shapes,
        in_specs=[vmem] * 3,
        out_specs=(anywhere,) * 3,
        scratch_shapes=[pltpu.SemaphoreType.DMA((3,))],
        compiler_params=pltpu.CompilerParams(vmem_limit_bytes=1024 * 1024),
        name="copy_out",
    )(*results)


def solution(mesh):
    in_specs = (P("group", "brick", None, None), P("group", "brick", None, None), P(), P())
    out_specs = (P("group", "brick", None, None), P(None, "brick", None), P(None, "brick", None))
    return jax.shard_map(body, mesh=mesh, in_specs=in_specs, out_specs=out_specs, check_vma=False)
```
